128 devices in a mesh: row: 16 (over x, y), col: 8 (over z, core).
Axes of the slice: x: 4, y: 4, z: 4, core: 2. Of those that a mesh axis runs over, the one named last changes fastest.
Arguments:
- tiles: bfloat16 [32768, 128, 128], P(('row', 'col'))
- tile_src: int32 [32768], P(('row', 'col')), may hold values from 0 to 15
- tile_slot: int32 [32768], P(('row', 'col')), may hold values from 0 to 127
- slot_block: int32 [16384], P(('row', 'col')), may hold values from 0 to 15
- out_degree: int32 [262144], P(('row', 'col')), may hold values from 512 to 2047
- good_seeds: int32 [128, 16384], P(None, ('row', 'col')), may hold values from 0 to 262143, as said below
- spam_cores: int32 [128, 8192], P(None, ('row', 'col')), may hold values from 0 to 262143, as said below
Outputs:
- trust: float32 [262144, 128], P(('row', 'col'))
- distrust: float32 [262144, 128], P(('row', 'col'))
The draws below stay inside these ranges and needn't reach their ends.
Inputs may be any that keep to these rules, and one draw needn't show every extreme that they name: `tile_slot`: slot s of a device belongs to the peer with index s // 1 along row+col. `slot_block`: entry p * 128 + s is the local index, among the 16 blocks held by peer s, of the target block of slot s of device p. `good_seeds`: entries j * 128 to (j + 1) * 128 - 1 of each column's list are hosts of device j, from j * 2048 to (j + 1) * 2048 - 1. `spam_cores`: entries j * 64 to (j + 1) * 64 - 1 of each column's list are hosts of device j, from j * 2048 to (j + 1) * 2048 - 1.
All inputs are finite; a program needn't handle non-finite values.
Results may differ from the reference program's by a relative error of at most 0.0003.
Values may be sent and summed in bfloat16 or wider, within the bound.
No kernel may reach another device: no remote copies, remote signals or barrier semaphores. Data moves between devices by JAX's collectives and lax.ppermute only.
A program may use at most 128 MiB of HBM per device.

```python
import math
import jax
import jax.numpy as jnp
import numpy as np
from jax import lax

BS = 128
S = 128
BLK_DEV = 16
TILES_DEV = 256
SLOTS_DEV = 128
TRUST_ITERS = 2
ANTI_ITERS = 2
CAP = 1
HOSTS_DEV = 2048
NB = 2048
HOSTS = 262144
NTILES = 32768
SLOTS = 16384
GOOD_DEV = 128
K_GOOD = 16384
SPAM_DEV = 64
K_SPAM = 8192
N_ROW = 16
N_COL = 8


def draw_tiles(key, part):
    first, second, third = jax.random.split(key, 3)
    base = 4.6 * jnp.exp(jax.random.uniform(first, (NTILES, BS, BS), jnp.float32, math.log(0.0001), 0.0))
    lower, upper = (0.3, 3.0)
    row_scale = jnp.exp(jax.random.uniform(second, (NTILES, BS, 1), jnp.float32, math.log(lower), math.log(upper)))
    column_scale = jnp.exp(jax.random.uniform(third, (NTILES, 1, BS), jnp.float32, math.log(lower), math.log(upper)))
    return (base * row_scale * column_scale).astype(jnp.bfloat16)


def local_hosts(key, per_device, total):
    local = jax.random.randint(key, (S, total), 0, HOSTS_DEV, dtype=jnp.int32)
    owner = (jnp.arange(total, dtype=jnp.int32) // per_device).astype(jnp.int32)
    return (local + owner[None, :] * HOSTS_DEV).astype(jnp.int32)


def draw_good_seeds(key, part):
    return local_hosts(jax.random.fold_in(key, 11), GOOD_DEV, K_GOOD)


def draw_spam_cores(key, part):
    return local_hosts(jax.random.fold_in(key, 23), SPAM_DEV, K_SPAM)


def plant(values, key, least, high):
    longest = values.shape.index(max(values.shape))
    spots = []
    for shift in (0, 1):
        where = [jax.random.randint(jax.random.fold_in(key, axis), (), 0, length) for axis, length in enumerate(values.shape)]
        where[longest] = (where[longest] + shift) % values.shape[longest]
        spots.append(tuple(where))
    return values.at[spots[0]].set(least).at[spots[1]].set(high)


def rank_table(count, lean):
    loads = [(1 << 20) // math.isqrt(grade ** lean) + 1 for grade in range(1, count + 1)]
    deviation = 1 + sum(loads) // (1 << 30)
    return np.cumsum(np.array([max(1, weight // deviation) for weight in loads]))


def ranked_ids(stream_key, shape, amount, slope):
    grid = rank_table(amount, slope)
    pick = jax.random.randint(jax.random.fold_in(stream_key, 1), shape, 0, int(grid[amount - 1]))
    standing = jnp.searchsorted(jnp.asarray(grid, jnp.int32), pick, side="right")
    return jax.random.permutation(jax.random.fold_in(stream_key, 2), amount)[standing].astype(jnp.int32)


def setup_inputs(seed: int = 0) -> dict:
    key_list = jax.random.split(jax.random.key(seed), 8)
    tiles = draw_tiles(jax.random.fold_in(key_list[7], 71), 0)
    tile_src = plant(jax.random.randint(key_list[1], (NTILES,), 0, BLK_DEV), jax.random.fold_in(key_list[1], 1), 0, BLK_DEV - 1).astype(jnp.int32)
    tile_slot = plant(jax.random.randint(key_list[2], (NTILES,), 0, SLOTS_DEV), jax.random.fold_in(key_list[2], 1), 0, SLOTS_DEV - 1).astype(jnp.int32)
    slot_block = plant(ranked_ids(key_list[3], (SLOTS,), BLK_DEV, 1), jax.random.fold_in(key_list[3], 3), 0, BLK_DEV - 1).astype(jnp.int32)
    out_degree = plant(jax.random.randint(key_list[4], (HOSTS,), TILES_DEV * BS // (4 * BLK_DEV), TILES_DEV * BS // BLK_DEV), jax.random.fold_in(key_list[4], 1), TILES_DEV * BS // (4 * BLK_DEV), (TILES_DEV * BS // BLK_DEV) - 1).astype(jnp.int32)
    good_seeds = draw_good_seeds(jax.random.fold_in(key_list[7], 71), 0)
    spam_cores = draw_spam_cores(jax.random.fold_in(key_list[7], 71), 0)
    return dict(tiles=tiles, tile_src=tile_src, tile_slot=tile_slot, slot_block=slot_block, out_degree=out_degree, good_seeds=good_seeds, spam_cores=spam_cores)


def teleport(seeds, factor):
    column_index = jnp.broadcast_to(jnp.arange(S, dtype=jnp.int32)[:, None], seeds.shape)
    counts = jnp.zeros((HOSTS, S), jnp.float32).at[seeds, column_index].add(jnp.float32(1.0))
    return counts * jnp.float32(factor)


def reference(tiles, tile_src, tile_slot, slot_block, out_degree, good_seeds, spam_cores):
    devices = N_ROW * N_COL
    owner = (jnp.arange(NTILES, dtype=jnp.int32) // TILES_DEV).astype(jnp.int32)
    source_block = (owner * BLK_DEV + tile_src).astype(jnp.int32)
    global_slot = (owner * SLOTS_DEV + tile_slot).astype(jnp.int32)
    target_block = ((tile_slot // CAP) * BLK_DEV + slot_block[global_slot]).astype(jnp.int32)
    column_sums = jnp.sum(tiles, axis=1, dtype=jnp.float32)
    in_weight = 1.0 + jax.ops.segment_sum(column_sums, target_block, num_segments=NB).reshape(HOSTS)
    good_start = teleport(good_seeds, HOSTS_DEV / GOOD_DEV)
    spam_start = teleport(spam_cores, HOSTS_DEV / SPAM_DEV)
    grouped = tiles.reshape(devices, TILES_DEV, BS, BS)
    source_groups = source_block.reshape(devices, TILES_DEV)
    target_groups = target_block.reshape(devices, TILES_DEV)

    def forward(scaled):
        blocks = scaled.reshape(NB, BS, S)

        def one_group(total, group):
            weights, sources, targets = group
            products = jnp.einsum("kij,kis->kjs", weights.astype(jnp.float32), blocks[sources].astype(jnp.float32), precision=lax.Precision.HIGHEST)
            return total + jax.ops.segment_sum(products, targets, num_segments=NB), None

        total, _ = lax.scan(one_group, jnp.zeros((NB, BS, S), jnp.float32), (grouped, source_groups, target_groups))
        return total.reshape(HOSTS, S)

    def backward(share):
        blocks = share.reshape(NB, BS, S)

        def one_group(total, group):
            weights, sources, targets = group
            products = jnp.einsum("kij,kjs->kis", weights.astype(jnp.float32), blocks[targets].astype(jnp.float32), precision=lax.Precision.HIGHEST)
            return total + jax.ops.segment_sum(products, sources, num_segments=NB), None

        total, _ = lax.scan(one_group, jnp.zeros((NB, BS, S), jnp.float32), (grouped, source_groups, target_groups))
        return total.reshape(HOSTS, S)

    degree = out_degree.astype(jnp.float32)[:, None]
    trust = good_start
    for iteration in range(TRUST_ITERS):
        scaled = (trust / degree).astype(jnp.bfloat16)
        trust = 0.85 * forward(scaled) + 0.15 * good_start
    shield = 1.0 / (1.0 + trust)
    distrust = spam_start
    for iteration in range(ANTI_ITERS):
        share = (shield * distrust / in_weight[:, None]).astype(jnp.bfloat16)
        distrust = 0.85 * backward(share) + 0.15 * spam_start
    return trust, distrust
```

```python
import functools

import jax
import jax.numpy as jnp
from jax import lax
from jax.experimental import pallas as pl
from jax.experimental.pallas import tpu as pltpu
from jax.sharding import PartitionSpec as P

AXES = ("row", "col")
F32, BF16, I16, I32 = jnp.float32, jnp.bfloat16, jnp.int16, jnp.int32
BS = 128
EXTRA = 8
LOG_TOP = 14.997
STEPS = 64.0
LEAST = 1e-30
FINE = 65000.0

ANY = pl.BlockSpec(memory_space=pl.ANY)
SMEM = pl.BlockSpec(memory_space=pltpu.SMEM)
VMEM = pl.BlockSpec(memory_space=pltpu.VMEM)


def params(mib):
    return pltpu.CompilerParams(vmem_limit_bytes=mib << 20)


def exchange(x):
    return lax.all_to_all(x, AXES, split_axis=0, concat_axis=0, tiled=True)


def fetch(hbm, vmem, sems, chunk):
    return [
        pltpu.make_async_copy(
            hbm.at[pl.ds(c * chunk, chunk)], vmem.at[pl.ds(c * chunk, chunk)], sems.at[c]
        )
        for c in range(hbm.shape[0] // chunk)
    ]


def histogram(seeds_ref, out_ref, factor):
    columns, depth = seeds_ref.shape
    blocks = out_ref.shape[0] // columns
    unroll = 8

    def group(g, _):
        for u in range(unroll):
            s = g * unroll + u
            local = seeds_ref[pl.ds(s, 1), :] & (blocks * BS - 1)
            high = (lax.broadcasted_iota(I32, (blocks, depth), 0) == (local >> 7)).astype(F32).astype(BF16)
            low = (lax.broadcasted_iota(I32, (BS, depth), 0) == (local & (BS - 1))).astype(F32).astype(BF16)
            count = lax.dot_general(high, low, (((1,), (1,)), ((), ())), preferred_element_type=F32)
            out_ref[pl.ds(s, blocks, stride=columns), :] = count * factor
        return 0

    lax.fori_loop(0, columns // unroll, group, 0)


def encode_scale(largest):
    return jnp.ceil(jnp.log2(jnp.maximum(largest, LEAST)) * STEPS)


def up(code):
    return jnp.exp2(LOG_TOP - code * (1.0 / STEPS))


def down(code):
    return jnp.exp2(code * (1.0 / STEPS) - LOG_TOP)


def to_i16(x):
    return jnp.round(x).astype(I32).astype(I16)


def push(x_ref, tile_copies, tiles, src, slot, acc, chunk):
    def clear(g, _):
        acc[g] = jnp.zeros(acc.shape[1:], F32)
        return 0

    lax.fori_loop(0, acc.shape[0], clear, 0)
    unroll = 8
    for c, copy in enumerate(tile_copies):
        copy.wait()

        def group(g, _):
            base = c * chunk + g * unroll
            parts = [
                jnp.dot(x_ref[src[base + u]], tiles[base + u], preferred_element_type=F32)
                for u in range(unroll)
            ]
            for u in range(unroll):
                at = slot[base + u]
                acc[at] = acc[at] + parts[u]
            return 0

        lax.fori_loop(0, chunk // unroll, group, 0)


def send(acc, extra_row, staged, out_hbm, sems, chunk):
    copies = []
    row = lax.broadcasted_iota(I32, (EXTRA, BS), 0)
    unroll = 4
    for c in range(acc.shape[0] // chunk):

        def group(g, _):
            for u in range(unroll):
                p = c * chunk + g * unroll + u
                block = acc[p]
                code = encode_scale(jnp.max(jnp.abs(block), axis=0, keepdims=True))
                staged[p, 0:BS, :] = to_i16(block * up(code))
                tail = jnp.where(row == 0, jnp.broadcast_to(code.astype(I32), (EXTRA, BS)), extra_row(p))
                staged[p, BS : BS + EXTRA, :] = tail.astype(I16)
            return 0

        lax.fori_loop(0, chunk // unroll, group, 0)
        copy = pltpu.make_async_copy(
            staged.at[pl.ds(c * chunk, chunk)], out_hbm.at[pl.ds(c * chunk, chunk)], sems.at[c]
        )
        copy.start()
        copies.append(copy)
    for copy in copies:
        copy.wait()


def receive(arrived, copies, ids, total, chunk, also=None):
    for b in range(total.shape[0]):
        total[b] = jnp.zeros(total.shape[1:], F32)
    unroll = 4
    for c, copy in enumerate(copies):
        copy.wait()

        def group(g, _):
            for u in range(unroll):
                p = c * chunk + g * unroll + u
                tail = arrived[p, BS : BS + EXTRA, :].astype(I32).astype(F32)
                values = arrived[p, 0:BS, :].astype(I32).astype(F32) * down(tail[0:1])
                at = ids[p]
                total[at] = total[at] + values
                if also is not None:
                    also(at, tail)
            return 0

        lax.fori_loop(0, chunk // unroll, group, 0)


def first_kernel(chunk, slots_chunk, factor, seeds, degree, src, slot, slot_block, tiles_hbm,
                 out_hbm, good, tiles, x, acc, staged, counts, tile_sems, out_sems):
    copies = fetch(tiles_hbm, tiles, tile_sems, chunk)
    for copy in copies:
        copy.start()
    histogram(seeds, counts, factor)
    blocks, columns = x.shape[0], x.shape[1]

    def scale(b, _):
        trust = counts[pl.ds(b * columns, columns), :]
        good[b] = trust.astype(BF16)
        x[b] = (trust / degree[b].astype(F32)).astype(BF16)
        return 0

    lax.fori_loop(0, blocks, scale, 0)
    push(x, copies, tiles, src, slot, acc, chunk)
    send(acc, lambda p: slot_block[p], staged, out_hbm, out_sems, slots_chunk)


def second_kernel(chunk, slots_chunk, ids, degree, src, slot, good, weights, arrived_hbm, tiles_hbm,
                  out_hbm, arrived, tiles, x, total, acc, staged, in_sems, tile_sems, out_sems):
    incoming = fetch(arrived_hbm, arrived, in_sems, slots_chunk)
    copies = fetch(tiles_hbm, tiles, tile_sems, chunk)
    for copy in incoming + copies:
        copy.start()
    receive(arrived, incoming, ids, total, slots_chunk)

    def scale(b, _):
        trust = 0.85 * total[b] + 0.15 * good[b].astype(F32)
        x[b] = (trust / degree[b].astype(F32)).astype(BF16)
        return 0

    lax.fori_loop(0, x.shape[0], scale, 0)
    push(x, copies, tiles, src, slot, acc, chunk)
    send(acc, lambda p: weights[p].astype(I32), staged, out_hbm, out_sems, slots_chunk)


def requests(share, ids, staged, out_hbm, sems, chunk):
    copies = []
    unroll = min(8, chunk)
    for c in range(staged.shape[0] // chunk):

        def group(g, _):
            for u in range(unroll):
                p = c * chunk + g * unroll + u
                staged[p] = share[ids[p]]
            return 0

        lax.fori_loop(0, chunk // unroll, group, 0)
        copy = pltpu.make_async_copy(
            staged.at[pl.ds(c * chunk, chunk)], out_hbm.at[pl.ds(c * chunk, chunk)], sems.at[c]
        )
        copy.start()
        copies.append(copy)
    for copy in copies:
        copy.wait()


def third_kernel(slots_chunk, ids, good, spam, arrived_hbm, out_hbm, trust, shield, in_weight,
                 arrived, total, share, staged, in_sems, out_sems):
    incoming = fetch(arrived_hbm, arrived, in_sems, slots_chunk)
    for copy in incoming:
        copy.start()
    blocks = total.shape[0]
    in_weight[...] = jnp.ones(in_weight.shape, F32)

    def add_weight(at, tail):
        value = (tail[2:3] + tail[3:4] * (1.0 / FINE)) * down(tail[1:2])
        in_weight[at] = in_weight[at] + value

    receive(arrived, incoming, ids, total, slots_chunk, add_weight)

    def finish(b, _):
        value = 0.85 * total[b] + 0.15 * good[b].astype(F32)
        trust[b] = value
        keep = 1.0 / (1.0 + value)
        shield[b] = keep
        share[b] = (keep * spam[b].astype(F32) / in_weight[b]).astype(BF16)
        return 0

    lax.fori_loop(0, blocks, finish, 0)
    requests(share, ids, staged, out_hbm, out_sems, slots_chunk)


def pull(y, incoming, tiles, copies, src, slot, total, chunk):
    for b in range(total.shape[0]):
        total[b] = jnp.zeros(total.shape[1:], F32)
    for copy in incoming:
        copy.wait()
    unroll = 8
    for c, copy in enumerate(copies):
        copy.wait()

        def group(g, _):
            base = c * chunk + g * unroll
            parts = [
                lax.dot_general(
                    y[slot[base + u]], tiles[base + u], (((1,), (1,)), ((), ())), preferred_element_type=F32
                )
                for u in range(unroll)
            ]
            for u in range(unroll):
                at = src[base + u]
                total[at] = total[at] + parts[u]
            return 0

        lax.fori_loop(0, chunk // unroll, group, 0)


def fourth_kernel(chunk, slots_chunk, ids, src, slot, spam, shield, in_weight, arrived_hbm, tiles_hbm, out_hbm,
                  arrived, tiles, total, share, staged, in_sems, tile_sems, out_sems):
    incoming = fetch(arrived_hbm, arrived, in_sems, slots_chunk)
    copies = fetch(tiles_hbm, tiles, tile_sems, chunk)
    for copy in incoming + copies:
        copy.start()
    pull(arrived, incoming, tiles, copies, src, slot, total, chunk)

    def finish(b, _):
        value = 0.85 * total[b] + 0.15 * spam[b].astype(F32)
        share[b] = (shield[b] * value / in_weight[b]).astype(BF16)
        return 0

    lax.fori_loop(0, share.shape[0], finish, 0)
    requests(share, ids, staged, out_hbm, out_sems, slots_chunk)


def fifth_kernel(chunk, slots_chunk, src, slot, spam, arrived_hbm, tiles_hbm, distrust,
                 arrived, tiles, total, in_sems, tile_sems):
    incoming = fetch(arrived_hbm, arrived, in_sems, slots_chunk)
    copies = fetch(tiles_hbm, tiles, tile_sems, chunk)
    for copy in incoming + copies:
        copy.start()
    pull(arrived, incoming, tiles, copies, src, slot, total, chunk)

    def finish(b, _):
        distrust[b] = jnp.transpose(0.85 * total[b] + 0.15 * spam[b].astype(F32))
        return 0

    lax.fori_loop(0, total.shape[0], finish, 0)


def turn_kernel(wide, tall):
    def turn(b, _):
        tall[b] = jnp.transpose(wide[b])
        return 0

    lax.fori_loop(0, wide.shape[0], turn, 0)


def side_kernel(chunk, factor, seeds, slot, tiles_hbm, spam, weights, tiles, counts, sums, tile_sems):
    copies = fetch(tiles_hbm, tiles, tile_sems, chunk)
    for copy in copies:
        copy.start()
    histogram(seeds, counts, factor)
    blocks, columns = spam.shape[0], spam.shape[1]

    def keep(b, _):
        spam[b] = counts[pl.ds(b * columns, columns), :].astype(BF16)
        return 0

    lax.fori_loop(0, blocks, keep, 0)
    sums[...] = jnp.zeros(sums.shape, F32)
    unroll = 4
    for c, copy in enumerate(copies):
        copy.wait()

        def group(g, _):
            for u in range(unroll):
                k = c * chunk + g * unroll + u
                at = slot[k]
                sums[at] = sums[at] + jnp.sum(tiles[k].astype(F32), axis=0, keepdims=True)
            return 0

        lax.fori_loop(0, chunk // unroll, group, 0)
    row = lax.broadcasted_iota(I32, (EXTRA, BS), 0)

    def pack(p, _):
        value = sums[p]
        code = encode_scale(jnp.abs(value))
        whole = value * up(code)
        coarse = jnp.round(whole)
        fine = jnp.round((whole - coarse) * FINE)
        wide = lambda v: jnp.broadcast_to(v, (EXTRA, BS)).astype(I32)
        tail = jnp.where(row == 1, wide(code), jnp.where(row == 2, wide(coarse), jnp.where(row == 3, wide(fine), 0)))
        weights[p] = tail.astype(I16)
        return 0

    lax.fori_loop(0, sums.shape[0], pack, 0)


def cost(flops, bytes_moved):
    return pl.CostEstimate(flops=flops, bytes_accessed=bytes_moved, transcendentals=0)


def body(tiles, tile_src, tile_slot, slot_block, out_degree, good_seeds, spam_cores):
    count, size = tiles.shape[0], tiles.shape[1]
    hosts = out_degree.shape[0]
    blocks = hosts // size
    columns = good_seeds.shape[0]
    slots = slot_block.shape[0]
    chunk, slots_chunk = min(16, count), min(16, slots)
    dma = pltpu.SemaphoreType.DMA
    tile_sems, slot_sems = dma((count // chunk,)), dma((slots // slots_chunk,))
    sds = jax.ShapeDtypeStruct
    sent = sds((slots, columns + EXTRA, size), I16)
    asked = sds((slots, columns, size), BF16)
    panel = (blocks, columns, size)
    tiles_buf = pltpu.VMEM(tiles.shape, BF16)
    sent_buf = pltpu.VMEM(sent.shape, I16)
    asked_buf = pltpu.VMEM(asked.shape, BF16)
    total_buf = pltpu.VMEM(panel, F32)
    half_buf = pltpu.VMEM(panel, BF16)
    acc_buf = pltpu.VMEM((slots, columns, size), F32)
    counts_buf = pltpu.VMEM((blocks * columns, size), F32)
    degree = out_degree.reshape(blocks, 1, size)
    work = 2 * count * size * size * columns
    tile_bytes = 2 * count * size * size

    outgoing, good = pl.pallas_call(
        functools.partial(first_kernel, chunk, slots_chunk, float(hosts / good_seeds.shape[1])),
        out_shape=(sent, sds(panel, BF16)),
        in_specs=[VMEM, VMEM, SMEM, SMEM, SMEM, ANY],
        out_specs=(ANY, VMEM),
        scratch_shapes=[tiles_buf, half_buf, acc_buf, sent_buf, counts_buf, tile_sems, slot_sems],
        compiler_params=params(56),
        cost_estimate=cost(work, 2 * tile_bytes),
        name="first_push",
    )(good_seeds, degree, tile_src, tile_slot, slot_block, tiles)
    arrived = exchange(outgoing)
    spam_seeds, slot_after, _ = lax.optimization_barrier((spam_cores, tile_slot, good))
    spam, weights = pl.pallas_call(
        functools.partial(side_kernel, chunk, float(hosts / spam_cores.shape[1])),
        out_shape=(sds(panel, BF16), sds((slots, EXTRA, size), I16)),
        in_specs=[VMEM, SMEM, ANY],
        out_specs=(VMEM, VMEM),
        scratch_shapes=[tiles_buf, counts_buf, pltpu.VMEM((slots, 1, size), F32), tile_sems],
        compiler_params=params(40),
        cost_estimate=cost(work // 4, tile_bytes),
        name="side",
    )(spam_seeds, slot_after, tiles)
    ids = arrived[:, columns + 1, 0].astype(I32)
    outgoing = pl.pallas_call(
        functools.partial(second_kernel, chunk, slots_chunk),
        out_shape=sent,
        in_specs=[SMEM, VMEM, SMEM, SMEM, VMEM, VMEM, ANY, ANY],
        out_specs=ANY,
        scratch_shapes=[sent_buf, tiles_buf, half_buf, total_buf, acc_buf, sent_buf, slot_sems, tile_sems, slot_sems],
        compiler_params=params(56),
        cost_estimate=cost(work, 2 * tile_bytes),
        name="second_push",
    )(ids, degree, tile_src, tile_slot, good, weights, arrived, tiles)
    arrived = exchange(outgoing)
    asked_for, trust, shield, in_weight = pl.pallas_call(
        functools.partial(third_kernel, slots_chunk),
        out_shape=(asked, sds(panel, F32), sds(panel, F32), sds((blocks, 1, size), F32)),
        in_specs=[SMEM, VMEM, VMEM, ANY],
        out_specs=(ANY, VMEM, VMEM, VMEM),
        scratch_shapes=[sent_buf, total_buf, half_buf, asked_buf, slot_sems, slot_sems],
        compiler_params=params(56),
        cost_estimate=cost(work // 8, tile_bytes),
        name="first_shares",
    )(ids, good, spam, arrived)
    arrived = exchange(asked_for)
    trust_out = pl.pallas_call(
        turn_kernel,
        out_shape=sds((blocks, size, columns), F32),
        in_specs=[VMEM],
        out_specs=VMEM,
        compiler_params=params(16),
        cost_estimate=cost(work // 64, tile_bytes // 4),
        name="turn",
    )(trust)
    asked_for = pl.pallas_call(
        functools.partial(fourth_kernel, chunk, slots_chunk),
        out_shape=asked,
        in_specs=[SMEM, SMEM, SMEM, VMEM, VMEM, VMEM, ANY, ANY],
        out_specs=ANY,
        scratch_shapes=[asked_buf, tiles_buf, total_buf, half_buf, asked_buf, slot_sems, tile_sems, slot_sems],
        compiler_params=params(56),
        cost_estimate=cost(work, 2 * tile_bytes),
        name="second_shares",
    )(ids, tile_src, tile_slot, spam, shield, in_weight, arrived, tiles)
    arrived = exchange(asked_for)
    distrust = pl.pallas_call(
        functools.partial(fifth_kernel, chunk, slots_chunk),
        out_shape=sds((blocks, size, columns), F32),
        in_specs=[SMEM, SMEM, VMEM, ANY, ANY],
        out_specs=VMEM,
        scratch_shapes=[asked_buf, tiles_buf, total_buf, slot_sems, tile_sems],
        compiler_params=params(56),
        cost_estimate=cost(work, 2 * tile_bytes),
        name="last_pull",
    )(tile_src, tile_slot, spam, arrived, tiles)
    return trust_out.reshape(hosts, columns), distrust.reshape(hosts, columns)


def solution(mesh):
    in_specs = (
        P(AXES, None, None),
        P(AXES),
        P(AXES),
        P(AXES),
        P(AXES),
        P(None, AXES),
        P(None, AXES),
    )
    out_specs = (P(AXES, None), P(AXES, None))
    return jax.shard_map(body, mesh=mesh, in_specs=in_specs, out_specs=out_specs, check_vma=False)
```

```python
import functools

import jax
import jax.numpy as jnp
from jax import lax
from jax.experimental import pallas as pl
from jax.experimental.pallas import tpu as pltpu
from jax.sharding import PartitionSpec as P

AXES = ("row", "col")
F32, BF16, I16, I32 = jnp.float32, jnp.bfloat16, jnp.int16, jnp.int32
BS = 128
EXTRA = 8
LOG_TOP = 14.997
STEPS = 64.0
LEAST = 1e-30
FINE = 65000.0

ANY = pl.BlockSpec(memory_space=pl.ANY)
SMEM = pl.BlockSpec(memory_space=pltpu.SMEM)
VMEM = pl.BlockSpec(memory_space=pltpu.VMEM)
HBM = pl.BlockSpec(memory_space=pltpu.HBM)


def params(mib):
    return pltpu.CompilerParams(vmem_limit_bytes=mib << 20)


def exchange(x):
    return lax.all_to_all(x, AXES, split_axis=0, concat_axis=0, tiled=True)


def fetch(hbm, vmem, sems, chunk):
    return [
        pltpu.make_async_copy(
            hbm.at[pl.ds(c * chunk, chunk)], vmem.at[pl.ds(c * chunk, chunk)], sems.at[c]
        )
        for c in range(hbm.shape[0] // chunk)
    ]


def run_chunks(copies, group):
    def step(c, _):
        for k, copy in enumerate(copies):

            @pl.when(c == k)
            def _():
                copy.wait()

        group(c)
        return 0

    lax.fori_loop(0, len(copies), step, 0)


def histogram(seeds_ref, out_ref, factor):
    columns, depth = seeds_ref.shape
    blocks = out_ref.shape[0] // columns
    unroll = 16

    def group(g, _):
        for u in range(unroll):
            s = g * unroll + u
            local = seeds_ref[pl.ds(s, 1), :] & (blocks * BS - 1)
            high = (lax.broadcasted_iota(I32, (blocks, depth), 0) == (local >> 7)).astype(F32).astype(BF16)
            low = (lax.broadcasted_iota(I32, (BS, depth), 0) == (local & (BS - 1))).astype(F32).astype(BF16)
            count = lax.dot_general(high, low, (((1,), (1,)), ((), ())), preferred_element_type=F32)
            out_ref[pl.ds(s, blocks, stride=columns), :] = count * factor
        return 0

    lax.fori_loop(0, columns // unroll, group, 0)


def encode_scale(largest):
    return jnp.ceil(jnp.log2(jnp.maximum(largest, LEAST)) * STEPS)


def up(code):
    return jnp.exp2(LOG_TOP - code * (1.0 / STEPS))


def down(code):
    return jnp.exp2(code * (1.0 / STEPS) - LOG_TOP)


def to_i16(x):
    return jnp.round(x).astype(I32).astype(I16)


def push(x_ref, tiles, copies, src, slot, acc):
    def clear(g, _):
        acc[g] = jnp.zeros(acc.shape[1:], F32)
        return 0

    lax.fori_loop(0, acc.shape[0], clear, 0)
    unroll = tiles.shape[0] // len(copies)

    def group(g):
        base = g * unroll
        parts = [
            jnp.dot(x_ref[src[base + u]], tiles[base + u], preferred_element_type=F32)
            for u in range(unroll)
        ]
        for u in range(unroll):
            at = slot[base + u]
            acc[at] = acc[at] + parts[u]

    run_chunks(copies, group)


def send(acc, extra_row, staged, out_hbm, sems, chunk):
    copies = []
    row = lax.broadcasted_iota(I32, (EXTRA, BS), 0)
    unroll = 4
    for c in range(acc.shape[0] // chunk):

        def group(g, _):
            for u in range(unroll):
                p = c * chunk + g * unroll + u
                block = acc[p]
                code = encode_scale(jnp.max(jnp.abs(block), axis=0, keepdims=True))
                staged[p, 0:BS, :] = to_i16(block * up(code))
                tail = jnp.where(row == 0, jnp.broadcast_to(code.astype(I32), (EXTRA, BS)), extra_row(p))
                staged[p, BS : BS + EXTRA, :] = tail.astype(I16)
            return 0

        lax.fori_loop(0, chunk // unroll, group, 0)
        copy = pltpu.make_async_copy(
            staged.at[pl.ds(c * chunk, chunk)], out_hbm.at[pl.ds(c * chunk, chunk)], sems.at[c]
        )
        copy.start()
        copies.append(copy)
    for copy in copies:
        copy.wait()


def receive(arrived, copies, ids, total, chunk, also=None):
    for b in range(total.shape[0]):
        total[b] = jnp.zeros(total.shape[1:], F32)
    unroll = min(8, chunk)
    for c, copy in enumerate(copies):
        if copy is not None:
            copy.wait()
        at_chunk = ids(c)

        def group(g, _):
            for u in range(unroll):
                one = g * unroll + u
                p = c * chunk + one
                tail = arrived[p, BS : BS + EXTRA, :].astype(I32).astype(F32)
                values = arrived[p, 0:BS, :].astype(I32).astype(F32) * down(tail[0:1])
                at = at_chunk(one)
                total[at] = total[at] + values
                if also is not None:
                    also(at, tail)
            return 0

        lax.fori_loop(0, chunk // unroll, group, 0)


def ids_in(ids):
    return lambda c: lambda one: ids[c, 0, one]


def first_kernel(slots_chunk, tiles_chunk, factor, src, slot, slot_block, seeds, degree, tiles_hbm,
                 out_hbm, good, x, tiles, counts, acc, staged, tile_sems, out_sems):
    copies = fetch(tiles_hbm, tiles, tile_sems, tiles_chunk)
    for copy in copies:
        copy.start()
    histogram(seeds, counts, factor)
    blocks, columns = x.shape[0], x.shape[1]

    def scale(b, _):
        trust = counts[pl.ds(b * columns, columns), :]
        good[b] = trust.astype(BF16)
        x[b] = (trust / degree[b].astype(F32)).astype(BF16)
        return 0

    lax.fori_loop(0, blocks, scale, 0)
    push(x, tiles, copies, src, slot, acc)
    send(acc, lambda p: slot_block[p], staged, out_hbm, out_sems, slots_chunk)


def second_kernel(slots_chunk, tiles_chunk, src, slot, degree, good, weights, arrived_hbm, tiles_hbm, out_hbm, ids_out,
                  arrived, tiles, x, total, acc, staged, ids, in_sems, tile_sems, id_sems, out_sems):
    incoming = fetch(arrived_hbm, arrived, in_sems, slots_chunk)
    copies = fetch(tiles_hbm, tiles, tile_sems, tiles_chunk)
    for copy in incoming + copies:
        copy.start()
    lane = lax.broadcasted_iota(I32, (1, BS), 1)
    moves = []

    def collect(c):
        incoming[c].wait()
        row = jnp.zeros((1, BS), I32)
        for u in range(slots_chunk):
            tail = arrived[c * slots_chunk + u, BS : BS + EXTRA, :].astype(I32)
            row = jnp.where(lane == u, tail[1:2], row)
        ids_out[c] = row
        move = pltpu.make_async_copy(ids_out.at[c], ids.at[c], id_sems.at[c])
        move.start()
        moves.append(move)

    chunks = len(incoming)
    for c in range(min(2, chunks)):
        collect(c)

    def ids_of(c):
        if c + 2 < chunks:
            collect(c + 2)
        moves[c].wait()
        return lambda one: ids[c, 0, one]

    receive(arrived, [None] * chunks, ids_of, total, slots_chunk)

    def scale(b, _):
        trust = 0.85 * total[b] + 0.15 * good[b].astype(F32)
        x[b] = (trust / degree[b].astype(F32)).astype(BF16)
        return 0

    lax.fori_loop(0, x.shape[0], scale, 0)
    push(x, tiles, copies, src, slot, acc)
    send(acc, lambda p: weights[p].astype(I32), staged, out_hbm, out_sems, slots_chunk)


def requests(share, ids, staged, out_hbm, sems, chunk):
    copies = []
    unroll = min(16, chunk)
    for c in range(staged.shape[0] // chunk):

        def group(g, _):
            for u in range(unroll):
                one = g * unroll + u
                staged[c * chunk + one] = share[ids[c, 0, one]]
            return 0

        lax.fori_loop(0, chunk // unroll, group, 0)
        copy = pltpu.make_async_copy(
            staged.at[pl.ds(c * chunk, chunk)], out_hbm.at[pl.ds(c * chunk, chunk)], sems.at[c]
        )
        copy.start()
        copies.append(copy)
    for copy in copies:
        copy.wait()


def third_kernel(slots_chunk, ids, good, spam, arrived_hbm, out_hbm, trust, shield, in_weight,
                 arrived, total, share, staged, in_sems, out_sems):
    incoming = fetch(arrived_hbm, arrived, in_sems, slots_chunk)
    for copy in incoming:
        copy.start()
    blocks = total.shape[0]
    in_weight[...] = jnp.ones(in_weight.shape, F32)

    def add_weight(at, tail):
        value = (tail[2:3] + tail[3:4] * (1.0 / FINE)) * down(tail[1:2])
        in_weight[at] = in_weight[at] + value

    receive(arrived, incoming, ids_in(ids), total, slots_chunk, add_weight)

    def finish(b, _):
        value = 0.85 * total[b] + 0.15 * good[b].astype(F32)
        trust[b] = value
        keep = 1.0 / (1.0 + value)
        shield[b] = keep
        share[b] = (keep * spam[b].astype(F32) / in_weight[b]).astype(BF16)
        return 0

    lax.fori_loop(0, blocks, finish, 0)
    requests(share, ids, staged, out_hbm, out_sems, slots_chunk)


def pack_kernel(pairs, tiles_hbm, out_hbm, tiles, staged, sem, out_sem):
    copy = pltpu.make_async_copy(tiles_hbm, tiles, sem)
    copy.start()
    copy.wait()
    size = tiles.shape[1]

    def turn(k, _):
        staged[k, 0:size, :] = jnp.transpose(tiles[pairs[1, k]])
        staged[k, size : 2 * size, :] = jnp.transpose(tiles[pairs[2, k]])
        return 0

    lax.fori_loop(0, staged.shape[0], turn, 0)
    back = pltpu.make_async_copy(staged, out_hbm, out_sem)
    back.start()
    back.wait()


def pull(slots_chunk, pairs, arrived_hbm, packed_hbm, y, packed, total, in_sems, pair_sems):
    incoming = fetch(arrived_hbm, y, in_sems, slots_chunk)
    unroll = packed.shape[0] // pair_sems.shape[0]
    copies = fetch(packed_hbm, packed, pair_sems, unroll)
    for copy in incoming + copies:
        copy.start()
    y[arrived_hbm.shape[0]] = jnp.zeros(y.shape[1:], BF16)
    for b in range(total.shape[0]):
        total[b] = jnp.zeros(total.shape[1:], F32)
    for copy in incoming:
        copy.wait()

    def group(g):
        parts = []
        for u in range(unroll):
            k = g * unroll + u
            left = jnp.concatenate([y[pairs[3, k]], y[pairs[4, k]]], axis=1)
            parts.append(jnp.dot(left, packed[k], preferred_element_type=F32))
        for u in range(unroll):
            at = pairs[0, g * unroll + u]
            total[at] = total[at] + parts[u]

    run_chunks(copies, group)


def fourth_kernel(slots_chunk, ids, pairs, spam, shield, in_weight, arrived_hbm, packed_hbm, out_hbm,
                  y, packed, total, share, staged, in_sems, pair_sems, out_sems):
    pull(slots_chunk, pairs, arrived_hbm, packed_hbm, y, packed, total, in_sems, pair_sems)

    def finish(b, _):
        value = 0.85 * total[b] + 0.15 * spam[b].astype(F32)
        share[b] = (shield[b] * value / in_weight[b]).astype(BF16)
        return 0

    lax.fori_loop(0, share.shape[0], finish, 0)
    requests(share, ids, staged, out_hbm, out_sems, slots_chunk)


def fifth_kernel(slots_chunk, pairs, spam, arrived_hbm, packed_hbm, distrust, y, packed, total, in_sems, pair_sems):
    pull(slots_chunk, pairs, arrived_hbm, packed_hbm, y, packed, total, in_sems, pair_sems)

    def finish(b, _):
        distrust[b] = jnp.transpose(0.85 * total[b] + 0.15 * spam[b].astype(F32))
        return 0

    lax.fori_loop(0, total.shape[0], finish, 0)


def turn_kernel(wide, tall):
    def turn(b, _):
        tall[b] = jnp.transpose(wide[b])
        return 0

    lax.fori_loop(0, wide.shape[0], turn, 0)


def side_kernel(factor, seeds, slot, tiles_hbm, spam, weights, tiles, counts, sums, sem):
    copy = pltpu.make_async_copy(tiles_hbm, tiles, sem)
    copy.start()
    histogram(seeds, counts, factor)
    blocks, columns = spam.shape[0], spam.shape[1]

    def keep(b, _):
        spam[b] = counts[pl.ds(b * columns, columns), :].astype(BF16)
        return 0

    lax.fori_loop(0, blocks, keep, 0)
    copy.wait()
    sums[...] = jnp.zeros(sums.shape, F32)
    unroll = 4

    def group(g, _):
        for u in range(unroll):
            k = g * unroll + u
            at = slot[k]
            sums[at] = sums[at] + jnp.sum(tiles[k].astype(F32), axis=0, keepdims=True)
        return 0

    lax.fori_loop(0, tiles.shape[0] // unroll, group, 0)
    row = lax.broadcasted_iota(I32, (EXTRA, BS), 0)

    def pack(p, _):
        value = sums[p]
        code = encode_scale(jnp.abs(value))
        whole = value * up(code)
        coarse = jnp.round(whole)
        fine = jnp.round((whole - coarse) * FINE)
        wide = lambda v: jnp.broadcast_to(v, (EXTRA, BS)).astype(I32)
        tail = jnp.where(row == 1, wide(code), jnp.where(row == 2, wide(coarse), jnp.where(row == 3, wide(fine), 0)))
        weights[p] = tail.astype(I16)
        return 0

    lax.fori_loop(0, sums.shape[0], pack, 0)


def cost(flops, bytes_moved):
    return pl.CostEstimate(flops=flops, bytes_accessed=bytes_moved, transcendentals=0)


def pair_up(tile_src, tile_slot, blocks, slots):
    count = tile_src.shape[0]
    pairs = (count + blocks) // 2
    k = jnp.arange(count, dtype=I32)
    same = tile_src[:, None] == tile_src[None, :]
    rank = jnp.sum((same & (k[None, :] < k[:, None])).astype(I32), axis=1)
    block = jnp.arange(blocks, dtype=I32)
    held = jnp.sum((tile_src[:, None] == block[None, :]).astype(I32), axis=0)
    halves = (held + 1) // 2
    first = jnp.sum(jnp.where(block[:, None] < block[None, :], halves[:, None], 0), axis=0)
    start = jnp.sum(jnp.where(tile_src[:, None] == block[None, :], first[None, :], 0), axis=1)
    place = start + rank // 2
    here = place[None, :] == jnp.arange(pairs, dtype=I32)[:, None]
    even = here & (rank % 2 == 0)[None, :]
    odd = here & (rank % 2 == 1)[None, :]
    pick = lambda mask, v: jnp.sum(jnp.where(mask, v[None, :], 0), axis=1)
    shifted = tile_slot - slots
    return jnp.stack(
        [pick(even, tile_src), pick(even, k), pick(odd, k), slots + pick(even, shifted), slots + pick(odd, shifted)]
    )


def cost(flops, bytes_moved):
    return pl.CostEstimate(flops=flops, bytes_accessed=bytes_moved, transcendentals=0)


def body(tiles, tile_src, tile_slot, slot_block, out_degree, good_seeds, spam_cores):
    count, size = tiles.shape[0], tiles.shape[1]
    hosts = out_degree.shape[0]
    blocks = hosts // size
    columns = good_seeds.shape[0]
    slots = slot_block.shape[0]
    slots_chunk = min(16, slots)
    chunks = slots // slots_chunk
    sems = pltpu.SemaphoreType.DMA((chunks,))
    sds = jax.ShapeDtypeStruct
    sent = pltpu.HBM((slots, columns + EXTRA, size), I16)
    asked = pltpu.HBM((slots, columns, size), BF16)
    ids_shape = sds((chunks, 1, size), I32)
    panel = (blocks, columns, size)
    sent_buf = pltpu.VMEM(sent.shape, I16)
    asked_buf = pltpu.VMEM(asked.shape, BF16)
    y_buf = pltpu.VMEM((slots + 1, columns, size), BF16)
    total_buf = pltpu.VMEM(panel, F32)
    half_buf = pltpu.VMEM(panel, BF16)
    acc_buf = pltpu.VMEM((slots, columns, size), F32)
    counts_buf = pltpu.VMEM((blocks * columns, size), F32)
    degree = out_degree.reshape(blocks, 1, size)
    work = 2 * count * size * size * columns
    tile_bytes = 2 * count * size * size
    tiles_chunk = min(32, count)
    tiles_buf = pltpu.VMEM(tiles.shape, BF16)
    tile_sems = pltpu.SemaphoreType.DMA((count // tiles_chunk,))
    couples = (count + blocks) // 2
    pair_sems = pltpu.SemaphoreType.DMA((next(n for n in (8, 5, 4, 2, 1) if couples % n == 0),))
    packed_shape = (couples, 2 * size, size)
    packed_buf = pltpu.VMEM(packed_shape, BF16)

    outgoing, good = pl.pallas_call(
        functools.partial(first_kernel, slots_chunk, tiles_chunk, float(hosts / good_seeds.shape[1])),
        out_shape=(sent, sds(panel, BF16)),
        in_specs=[SMEM, SMEM, SMEM, VMEM, VMEM, ANY],
        out_specs=(HBM, VMEM),
        scratch_shapes=[half_buf, tiles_buf, counts_buf, acc_buf, sent_buf, tile_sems, sems],
        compiler_params=params(57),
        cost_estimate=cost(work, 2 * tile_bytes),
        name="first_push",
    )(tile_src, tile_slot, slot_block, good_seeds, degree, tiles)
    arrived = exchange(outgoing)
    spam_seeds, src_after, slot_after, _ = lax.optimization_barrier((spam_cores, tile_src, tile_slot, outgoing))
    spam, weights = pl.pallas_call(
        functools.partial(side_kernel, float(hosts / spam_cores.shape[1])),
        out_shape=(sds(panel, BF16), sds((slots, EXTRA, size), I16)),
        in_specs=[VMEM, SMEM, ANY],
        out_specs=(VMEM, VMEM),
        scratch_shapes=[tiles_buf, counts_buf, pltpu.VMEM((slots, 1, size), F32), pltpu.SemaphoreType.DMA],
        compiler_params=params(57),
        cost_estimate=cost(work // 4, tile_bytes),
        name="side",
    )(spam_seeds, slot_after, tiles)
    pairs = pair_up(src_after, slot_after, blocks, slots)
    outgoing, ids = pl.pallas_call(
        functools.partial(second_kernel, slots_chunk, tiles_chunk),
        out_shape=(sent, ids_shape),
        in_specs=[SMEM, SMEM, VMEM, VMEM, VMEM, HBM, ANY],
        out_specs=(HBM, VMEM),
        scratch_shapes=[
            sent_buf, tiles_buf, half_buf, total_buf, acc_buf, sent_buf, pltpu.SMEM(ids_shape.shape, I32),
            sems, tile_sems, sems, sems,
        ],
        compiler_params=params(57),
        cost_estimate=cost(work, 2 * tile_bytes),
        name="second_push",
    )(tile_src, tile_slot, degree, good, weights, arrived, tiles)
    arrived = exchange(outgoing)
    pairs_after, _ = lax.optimization_barrier((pairs, outgoing))
    packed = pl.pallas_call(
        pack_kernel,
        out_shape=pltpu.HBM(packed_shape, BF16),
        in_specs=[SMEM, ANY],
        out_specs=HBM,
        scratch_shapes=[tiles_buf, packed_buf, pltpu.SemaphoreType.DMA, pltpu.SemaphoreType.DMA],
        compiler_params=params(57),
        cost_estimate=cost(work // 4, 2 * tile_bytes),
        name="pack",
    )(pairs_after, tiles)
    asked_for, trust, shield, in_weight = pl.pallas_call(
        functools.partial(third_kernel, slots_chunk),
        out_shape=(asked, sds(panel, F32), sds(panel, F32), sds((blocks, 1, size), F32)),
        in_specs=[SMEM, VMEM, VMEM, HBM],
        out_specs=(HBM, VMEM, VMEM, VMEM),
        scratch_shapes=[sent_buf, total_buf, half_buf, asked_buf, sems, sems],
        compiler_params=params(57),
        cost_estimate=cost(work // 8, tile_bytes),
        name="first_shares",
    )(ids, good, spam, arrived)
    arrived = exchange(asked_for)
    trust_out = pl.pallas_call(
        turn_kernel,
        out_shape=sds((blocks, size, columns), F32),
        in_specs=[VMEM],
        out_specs=VMEM,
        compiler_params=params(16),
        cost_estimate=cost(work // 64, tile_bytes // 4),
        name="turn",
    )(trust)
    asked_for = pl.pallas_call(
        functools.partial(fourth_kernel, slots_chunk),
        out_shape=asked,
        in_specs=[SMEM, SMEM, VMEM, VMEM, VMEM, HBM, HBM],
        out_specs=HBM,
        scratch_shapes=[y_buf, packed_buf, total_buf, half_buf, asked_buf, sems, pair_sems, sems],
        compiler_params=params(57),
        cost_estimate=cost(work, 2 * tile_bytes),
        name="second_shares",
    )(ids, pairs, spam, shield, in_weight, arrived, packed)
    arrived = exchange(asked_for)
    distrust = pl.pallas_call(
        functools.partial(fifth_kernel, slots_chunk),
        out_shape=sds((blocks, size, columns), F32),
        in_specs=[SMEM, VMEM, HBM, HBM],
        out_specs=VMEM,
        scratch_shapes=[y_buf, packed_buf, total_buf, sems, pair_sems],
        compiler_params=params(57),
        cost_estimate=cost(work, 2 * tile_bytes),
        name="last_pull",
    )(pairs, spam, arrived, packed)
    return trust_out.reshape(hosts, columns), distrust.reshape(hosts, columns)


def solution(mesh):
    in_specs = (
        P(AXES, None, None),
        P(AXES),
        P(AXES),
        P(AXES),
        P(AXES),
        P(None, AXES),
        P(None, AXES),
    )
    out_specs = (P(AXES, None), P(AXES, None))
    return jax.shard_map(body, mesh=mesh, in_specs=in_specs, out_specs=out_specs, check_vma=False)
```

```python
import functools

import jax
import jax.numpy as jnp
from jax import lax
from jax.experimental import pallas as pl
from jax.experimental.pallas import tpu as pltpu
from jax.sharding import PartitionSpec as P

AXES = ("row", "col")
F32, BF16, I16, I32 = jnp.float32, jnp.bfloat16, jnp.int16, jnp.int32
BS = 128
EXTRA = 8
LOG_TOP = 14.997
STEPS = 64.0
LEAST = 1e-30
FINE = 65000.0

ANY = pl.BlockSpec(memory_space=pl.ANY)
SMEM = pl.BlockSpec(memory_space=pltpu.SMEM)
VMEM = pl.BlockSpec(memory_space=pltpu.VMEM)
HBM = pl.BlockSpec(memory_space=pltpu.HBM)


def params(mib):
    return pltpu.CompilerParams(vmem_limit_bytes=mib << 20)


def held(x):
    return pltpu.with_memory_space_constraint(x, pltpu.HBM)


def exchange(x):
    return lax.all_to_all(x, AXES, split_axis=0, concat_axis=0, tiled=True)


def fetch(hbm, vmem, sems, chunk):
    return [
        pltpu.make_async_copy(
            hbm.at[pl.ds(c * chunk, chunk)], vmem.at[pl.ds(c * chunk, chunk)], sems.at[c]
        )
        for c in range(hbm.shape[0] // chunk)
    ]


def run_chunks(copies, group):
    def step(c, _):
        for k, copy in enumerate(copies):

            @pl.when(c == k)
            def _():
                copy.wait()

        group(c)
        return 0

    lax.fori_loop(0, len(copies), step, 0)


def histogram(seeds_ref, out_ref, factor):
    columns, depth = seeds_ref.shape
    blocks = out_ref.shape[0] // columns
    unroll = 8
    none = jnp.zeros((blocks, depth), BF16)

    def group(g, _):
        for u in range(unroll):
            s = (g * unroll + u) * 2
            highs, lows = [], []
            for one in range(2):
                local = seeds_ref[pl.ds(s + one, 1), :] & (blocks * BS - 1)
                highs.append((lax.broadcasted_iota(I32, (blocks, depth), 0) == (local >> 7)).astype(F32).astype(BF16))
                lows.append((lax.broadcasted_iota(I32, (BS, depth), 0) == (local & (BS - 1))).astype(F32).astype(BF16))
            left = jnp.concatenate(
                [jnp.concatenate([highs[0], none], axis=1), jnp.concatenate([none, highs[1]], axis=1)], axis=0
            )
            count = lax.dot_general(
                left, jnp.concatenate(lows, axis=1), (((1,), (1,)), ((), ())), preferred_element_type=F32
            )
            for one in range(2):
                out_ref[pl.ds(s + one, blocks, stride=columns), :] = count[one * blocks : (one + 1) * blocks] * factor
        return 0

    lax.fori_loop(0, columns // (2 * unroll), group, 0)


def encode_scale(largest):
    return jnp.ceil(jnp.log2(jnp.maximum(largest, LEAST)) * STEPS)


def up(code):
    return jnp.exp2(LOG_TOP - code * (1.0 / STEPS))


def down(code):
    return jnp.exp2(code * (1.0 / STEPS) - LOG_TOP)


def to_i16(x):
    return jnp.round(x).astype(I32).astype(I16)


def push(x_ref, tiles, copies, src, slot, acc):
    def clear(g, _):
        acc[g] = jnp.zeros(acc.shape[1:], F32)
        return 0

    lax.fori_loop(0, acc.shape[0], clear, 0, unroll=4)
    unroll = tiles.shape[0] // len(copies)

    def group(g):
        base = g * unroll
        parts = [
            jnp.dot(x_ref[src[base + u]], tiles[base + u], preferred_element_type=F32)
            for u in range(unroll)
        ]
        for u in range(unroll):
            at = slot[base + u]
            acc[at] = acc[at] + parts[u]

    run_chunks(copies, group)


def send(acc, extra_row, staged, out_hbm, sems, chunk):
    copies = []
    row = lax.broadcasted_iota(I32, (EXTRA, BS), 0)
    unroll = min(8, chunk)
    for c in range(acc.shape[0] // chunk):

        def group(g, _):
            for u in range(unroll):
                p = c * chunk + g * unroll + u
                block = acc[p]
                code = encode_scale(jnp.max(jnp.abs(block), axis=0, keepdims=True))
                staged[p, 0:BS, :] = to_i16(block * up(code))
                tail = jnp.where(row == 0, jnp.broadcast_to(code.astype(I32), (EXTRA, BS)), extra_row(p))
                staged[p, BS : BS + EXTRA, :] = tail.astype(I16)
            return 0

        lax.fori_loop(0, chunk // unroll, group, 0)
        copy = pltpu.make_async_copy(
            staged.at[pl.ds(c * chunk, chunk)], out_hbm.at[pl.ds(c * chunk, chunk)], sems.at[c]
        )
        copy.start()
        copies.append(copy)
    for copy in copies:
        copy.wait()


def receive(arrived, copies, ids, total, chunk, also=None):
    for b in range(total.shape[0]):
        total[b] = jnp.zeros(total.shape[1:], F32)
    unroll = min(16, chunk)
    for c, copy in enumerate(copies):
        if copy is not None:
            copy.wait()
        at_chunk = ids(c)

        def group(g, _):
            for u in range(unroll):
                one = g * unroll + u
                p = c * chunk + one
                tail = arrived[p, BS : BS + EXTRA, :].astype(I32).astype(F32)
                values = arrived[p, 0:BS, :].astype(I32).astype(F32) * down(tail[0:1])
                at = at_chunk(one)
                total[at] = total[at] + values
                if also is not None:
                    also(at, tail)
            return 0

        lax.fori_loop(0, chunk // unroll, group, 0)


def ids_in(ids):
    return lambda c: lambda one: ids[c, 0, one]


def first_kernel(slots_chunk, tiles_chunk, factor, src, slot, slot_block, seeds, degree, tiles_hbm,
                 out_hbm, good, x, tiles, counts, acc, staged, tile_sems, out_sems):
    copies = fetch(tiles_hbm, tiles, tile_sems, tiles_chunk)
    for copy in copies:
        copy.start()
    histogram(seeds, counts, factor)
    blocks, columns = x.shape[0], x.shape[1]

    def scale(b, _):
        trust = counts[pl.ds(b * columns, columns), :]
        good[b] = trust.astype(BF16)
        x[b] = (trust / degree[b].astype(F32)).astype(BF16)
        return 0

    lax.fori_loop(0, blocks, scale, 0, unroll=4)
    push(x, tiles, copies, src, slot, acc)
    send(acc, lambda p: slot_block[p], staged, out_hbm, out_sems, slots_chunk)


def second_kernel(slots_chunk, tiles_chunk, src, slot, degree, good, weights, arrived_hbm, tiles_hbm, out_hbm, ids_out,
                  arrived, tiles, x, total, acc, staged, ids, in_sems, tile_sems, id_sems, out_sems):
    incoming = fetch(arrived_hbm, arrived, in_sems, slots_chunk)
    copies = fetch(tiles_hbm, tiles, tile_sems, tiles_chunk)
    for copy in incoming + copies:
        copy.start()
    lane = lax.broadcasted_iota(I32, (1, BS), 1)
    moves = []

    def collect(c):
        incoming[c].wait()
        row = jnp.zeros((1, BS), I32)
        for u in range(slots_chunk):
            tail = arrived[c * slots_chunk + u, BS : BS + EXTRA, :].astype(I32)
            row = jnp.where(lane == u, tail[1:2], row)
        ids_out[c] = row
        move = pltpu.make_async_copy(ids_out.at[c], ids.at[c], id_sems.at[c])
        move.start()
        moves.append(move)

    chunks = len(incoming)
    for c in range(min(2, chunks)):
        collect(c)

    def ids_of(c):
        if c + 2 < chunks:
            collect(c + 2)
        moves[c].wait()
        return lambda one: ids[c, 0, one]

    receive(arrived, [None] * chunks, ids_of, total, slots_chunk)

    def scale(b, _):
        trust = 0.85 * total[b] + 0.15 * good[b].astype(F32)
        x[b] = (trust / degree[b].astype(F32)).astype(BF16)
        return 0

    lax.fori_loop(0, x.shape[0], scale, 0, unroll=4)
    push(x, tiles, copies, src, slot, acc)
    send(acc, lambda p: weights[p].astype(I32), staged, out_hbm, out_sems, slots_chunk)


def requests(share, ids, staged, out_hbm, sems, chunk):
    copies = []
    unroll = min(16, chunk)
    for c in range(staged.shape[0] // chunk):

        def group(g, _):
            for u in range(unroll):
                one = g * unroll + u
                staged[c * chunk + one] = share[ids[c, 0, one]]
            return 0

        lax.fori_loop(0, chunk // unroll, group, 0)
        copy = pltpu.make_async_copy(
            staged.at[pl.ds(c * chunk, chunk)], out_hbm.at[pl.ds(c * chunk, chunk)], sems.at[c]
        )
        copy.start()
        copies.append(copy)
    for copy in copies:
        copy.wait()


def third_kernel(slots_chunk, ids, good, spam, arrived_hbm, out_hbm, trust, shield, in_weight,
                 arrived, total, share, staged, in_sems, out_sems):
    incoming = fetch(arrived_hbm, arrived, in_sems, slots_chunk)
    for copy in incoming:
        copy.start()
    blocks = total.shape[0]
    in_weight[...] = jnp.ones(in_weight.shape, F32)

    def add_weight(at, tail):
        value = (tail[2:3] + tail[3:4] * (1.0 / FINE)) * down(tail[1:2])
        in_weight[at] = in_weight[at] + value

    receive(arrived, incoming, ids_in(ids), total, slots_chunk, add_weight)

    def finish(b, _):
        value = 0.85 * total[b] + 0.15 * good[b].astype(F32)
        trust[b] = value
        keep = 1.0 / (1.0 + value)
        shield[b] = keep
        share[b] = (keep * spam[b].astype(F32) / in_weight[b]).astype(BF16)
        return 0

    lax.fori_loop(0, blocks, finish, 0, unroll=4)
    requests(share, ids, staged, out_hbm, out_sems, slots_chunk)


def pack_kernel(pairs, tiles_hbm, out_hbm, tiles, staged, sem, out_sem):
    copy = pltpu.make_async_copy(tiles_hbm, tiles, sem)
    copy.start()
    copy.wait()
    size = tiles.shape[1]

    def turn(k, _):
        staged[k, 0:size, :] = jnp.transpose(tiles[pairs[1, k]])
        staged[k, size : 2 * size, :] = jnp.transpose(tiles[pairs[2, k]])
        return 0

    lax.fori_loop(0, staged.shape[0], turn, 0)
    back = pltpu.make_async_copy(staged, out_hbm, out_sem)
    back.start()
    back.wait()


def pull(slots_chunk, pairs, arrived_hbm, packed_hbm, y, packed, total, in_sems, pair_sems):
    incoming = fetch(arrived_hbm, y, in_sems, slots_chunk)
    unroll = packed.shape[0] // pair_sems.shape[0]
    copies = fetch(packed_hbm, packed, pair_sems, unroll)
    for copy in incoming:
        copy.start(priority=0)
    for copy in copies:
        copy.start(priority=1)
    y[arrived_hbm.shape[0]] = jnp.zeros(y.shape[1:], BF16)
    for b in range(total.shape[0]):
        total[b] = jnp.zeros(total.shape[1:], F32)
    for copy in incoming:
        copy.wait()

    def group(g):
        parts = []
        for u in range(unroll):
            k = g * unroll + u
            left = jnp.concatenate([y[pairs[3, k]], y[pairs[4, k]]], axis=1)
            parts.append(jnp.dot(left, packed[k], preferred_element_type=F32))
        for u in range(unroll):
            at = pairs[0, g * unroll + u]
            total[at] = total[at] + parts[u]

    run_chunks(copies, group)


def fourth_kernel(slots_chunk, ids, pairs, spam, shield, in_weight, arrived_hbm, packed_hbm, out_hbm,
                  y, packed, total, share, staged, in_sems, pair_sems, out_sems):
    pull(slots_chunk, pairs, arrived_hbm, packed_hbm, y, packed, total, in_sems, pair_sems)

    def finish(b, _):
        value = 0.85 * total[b] + 0.15 * spam[b].astype(F32)
        share[b] = (shield[b] * value / in_weight[b]).astype(BF16)
        return 0

    lax.fori_loop(0, share.shape[0], finish, 0, unroll=4)
    requests(share, ids, staged, out_hbm, out_sems, slots_chunk)


def fifth_kernel(slots_chunk, pairs, spam, arrived_hbm, packed_hbm, distrust, y, packed, total, in_sems, pair_sems):
    pull(slots_chunk, pairs, arrived_hbm, packed_hbm, y, packed, total, in_sems, pair_sems)

    def finish(b, _):
        distrust[b] = jnp.transpose(0.85 * total[b] + 0.15 * spam[b].astype(F32))
        return 0

    lax.fori_loop(0, total.shape[0], finish, 0, unroll=4)


def turn_kernel(wide, tall):
    def turn(b, _):
        tall[b] = jnp.transpose(wide[b])
        return 0

    lax.fori_loop(0, wide.shape[0], turn, 0)


def side_kernel(factor, seeds, slot, tiles_hbm, spam, weights, tiles, counts, sums, sem):
    copy = pltpu.make_async_copy(tiles_hbm, tiles, sem)
    copy.start()
    histogram(seeds, counts, factor)
    blocks, columns = spam.shape[0], spam.shape[1]

    def keep(b, _):
        spam[b] = counts[pl.ds(b * columns, columns), :].astype(BF16)
        return 0

    lax.fori_loop(0, blocks, keep, 0)
    copy.wait()
    sums[...] = jnp.zeros(sums.shape, F32)
    unroll = 4

    def group(g, _):
        for u in range(unroll):
            k = g * unroll + u
            at = slot[k]
            sums[at] = sums[at] + jnp.sum(tiles[k].astype(F32), axis=0, keepdims=True)
        return 0

    lax.fori_loop(0, tiles.shape[0] // unroll, group, 0)
    row = lax.broadcasted_iota(I32, (EXTRA, BS), 0)

    def pack(p, _):
        value = sums[p]
        code = encode_scale(jnp.abs(value))
        whole = value * up(code)
        coarse = jnp.round(whole)
        fine = jnp.round((whole - coarse) * FINE)
        wide = lambda v: jnp.broadcast_to(v, (EXTRA, BS)).astype(I32)
        tail = jnp.where(row == 1, wide(code), jnp.where(row == 2, wide(coarse), jnp.where(row == 3, wide(fine), 0)))
        weights[p] = tail.astype(I16)
        return 0

    lax.fori_loop(0, sums.shape[0], pack, 0)


def cost(flops, bytes_moved):
    return pl.CostEstimate(flops=flops, bytes_accessed=bytes_moved, transcendentals=0)


def pair_up(tile_src, tile_slot, blocks, slots):
    count = tile_src.shape[0]
    pairs = (count + blocks) // 2
    k = jnp.arange(count, dtype=I32)
    same = tile_src[:, None] == tile_src[None, :]
    rank = jnp.sum((same & (k[None, :] < k[:, None])).astype(I32), axis=1)
    block = jnp.arange(blocks, dtype=I32)
    held = jnp.sum((tile_src[:, None] == block[None, :]).astype(I32), axis=0)
    halves = (held + 1) // 2
    first = jnp.sum(jnp.where(block[:, None] < block[None, :], halves[:, None], 0), axis=0)
    start = jnp.sum(jnp.where(tile_src[:, None] == block[None, :], first[None, :], 0), axis=1)
    place = start + rank // 2
    here = place[None, :] == jnp.arange(pairs, dtype=I32)[:, None]
    even = here & (rank % 2 == 0)[None, :]
    odd = here & (rank % 2 == 1)[None, :]
    pick = lambda mask, v: jnp.sum(jnp.where(mask, v[None, :], 0), axis=1)
    shifted = tile_slot - slots
    return jnp.stack(
        [pick(even, tile_src), pick(even, k), pick(odd, k), slots + pick(even, shifted), slots + pick(odd, shifted)]
    )


def cost(flops, bytes_moved):
    return pl.CostEstimate(flops=flops, bytes_accessed=bytes_moved, transcendentals=0)


def body(tiles, tile_src, tile_slot, slot_block, out_degree, good_seeds, spam_cores):
    count, size = tiles.shape[0], tiles.shape[1]
    hosts = out_degree.shape[0]
    blocks = hosts // size
    columns = good_seeds.shape[0]
    slots = slot_block.shape[0]
    slots_chunk = min(16, slots)
    chunks = slots // slots_chunk
    sems = pltpu.SemaphoreType.DMA((chunks,))
    sds = jax.ShapeDtypeStruct
    sent = pltpu.HBM((slots, columns + EXTRA, size), I16)
    asked = pltpu.HBM((slots, columns, size), BF16)
    ids_shape = sds((chunks, 1, size), I32)
    panel = (blocks, columns, size)
    sent_buf = pltpu.VMEM(sent.shape, I16)
    asked_buf = pltpu.VMEM(asked.shape, BF16)
    y_buf = pltpu.VMEM((slots + 1, columns, size), BF16)
    total_buf = pltpu.VMEM(panel, F32)
    half_buf = pltpu.VMEM(panel, BF16)
    acc_buf = pltpu.VMEM((slots, columns, size), F32)
    counts_buf = pltpu.VMEM((blocks * columns, size), F32)
    degree = out_degree.reshape(blocks, 1, size)
    work = 2 * count * size * size * columns
    tile_bytes = 2 * count * size * size
    tiles_chunk = min(128, count)
    tiles_buf = pltpu.VMEM(tiles.shape, BF16)
    tile_sems = pltpu.SemaphoreType.DMA((count // tiles_chunk,))
    couples = (count + blocks) // 2
    pair_sems = pltpu.SemaphoreType.DMA((next(n for n in (4, 5, 2, 1) if couples % n == 0),))
    packed_shape = (couples, 2 * size, size)
    packed_buf = pltpu.VMEM(packed_shape, BF16)

    outgoing, good = pl.pallas_call(
        functools.partial(first_kernel, slots_chunk, tiles_chunk, float(hosts / good_seeds.shape[1])),
        out_shape=(sent, sds(panel, BF16)),
        in_specs=[SMEM, SMEM, SMEM, VMEM, VMEM, ANY],
        out_specs=(HBM, VMEM),
        scratch_shapes=[half_buf, tiles_buf, counts_buf, acc_buf, sent_buf, tile_sems, sems],
        compiler_params=params(40),
        cost_estimate=cost(work, 2 * tile_bytes),
        name="first_push",
    )(tile_src, tile_slot, slot_block, good_seeds, degree, held(tiles))
    arrived = exchange(outgoing)
    spam_seeds, src_after, slot_after, _ = lax.optimization_barrier((spam_cores, tile_src, tile_slot, outgoing))
    spam, weights = pl.pallas_call(
        functools.partial(side_kernel, float(hosts / spam_cores.shape[1])),
        out_shape=(sds(panel, BF16), sds((slots, EXTRA, size), I16)),
        in_specs=[VMEM, SMEM, ANY],
        out_specs=(VMEM, VMEM),
        scratch_shapes=[tiles_buf, counts_buf, pltpu.VMEM((slots, 1, size), F32), pltpu.SemaphoreType.DMA],
        compiler_params=params(40),
        cost_estimate=cost(work // 4, tile_bytes),
        name="side",
    )(spam_seeds, slot_after, held(tiles))
    pairs = pair_up(src_after, slot_after, blocks, slots)
    outgoing, ids = pl.pallas_call(
        functools.partial(second_kernel, slots_chunk, tiles_chunk),
        out_shape=(sent, ids_shape),
        in_specs=[SMEM, SMEM, VMEM, VMEM, VMEM, HBM, ANY],
        out_specs=(HBM, VMEM),
        scratch_shapes=[
            sent_buf, tiles_buf, half_buf, total_buf, acc_buf, sent_buf, pltpu.SMEM(ids_shape.shape, I32),
            sems, tile_sems, sems, sems,
        ],
        compiler_params=params(40),
        cost_estimate=cost(work, 2 * tile_bytes),
        name="second_push",
    )(tile_src, tile_slot, degree, good, weights, held(arrived), held(tiles))
    arrived = exchange(outgoing)
    pairs_after, _ = lax.optimization_barrier((pairs, outgoing))
    packed = pl.pallas_call(
        pack_kernel,
        out_shape=pltpu.HBM(packed_shape, BF16),
        in_specs=[SMEM, ANY],
        out_specs=HBM,
        scratch_shapes=[tiles_buf, packed_buf, pltpu.SemaphoreType.DMA, pltpu.SemaphoreType.DMA],
        compiler_params=params(40),
        cost_estimate=cost(work // 4, 2 * tile_bytes),
        name="pack",
    )(pairs_after, held(tiles))
    asked_for, trust, shield, in_weight = pl.pallas_call(
        functools.partial(third_kernel, slots_chunk),
        out_shape=(asked, sds(panel, F32), sds(panel, F32), sds((blocks, 1, size), F32)),
        in_specs=[SMEM, VMEM, VMEM, HBM],
        out_specs=(HBM, VMEM, VMEM, VMEM),
        scratch_shapes=[sent_buf, total_buf, half_buf, asked_buf, sems, sems],
        compiler_params=params(40),
        cost_estimate=cost(work // 8, tile_bytes),
        name="first_shares",
    )(ids, good, spam, held(arrived))
    arrived = exchange(asked_for)
    trust_out = pl.pallas_call(
        turn_kernel,
        out_shape=sds((blocks, size, columns), F32),
        in_specs=[VMEM],
        out_specs=VMEM,
        compiler_params=params(16),
        cost_estimate=cost(work // 64, tile_bytes // 4),
        name="turn",
    )(trust)
    asked_for = pl.pallas_call(
        functools.partial(fourth_kernel, slots_chunk),
        out_shape=asked,
        in_specs=[SMEM, SMEM, VMEM, VMEM, VMEM, HBM, HBM],
        out_specs=HBM,
        scratch_shapes=[y_buf, packed_buf, total_buf, half_buf, asked_buf, sems, pair_sems, sems],
        compiler_params=params(40),
        cost_estimate=cost(work, 2 * tile_bytes),
        name="second_shares",
    )(ids, pairs, spam, shield, in_weight, held(arrived), held(packed))
    arrived = exchange(asked_for)
    distrust = pl.pallas_call(
        functools.partial(fifth_kernel, slots_chunk),
        out_shape=sds((blocks, size, columns), F32),
        in_specs=[SMEM, VMEM, HBM, HBM],
        out_specs=VMEM,
        scratch_shapes=[y_buf, packed_buf, total_buf, sems, pair_sems],
        compiler_params=params(40),
        cost_estimate=cost(work, 2 * tile_bytes),
        name="last_pull",
    )(pairs, spam, held(arrived), held(packed))
    return trust_out.reshape(hosts, columns), distrust.reshape(hosts, columns)


def solution(mesh):
    in_specs = (
        P(AXES, None, None),
        P(AXES),
        P(AXES),
        P(AXES),
        P(AXES),
        P(None, AXES),
        P(None, AXES),
    )
    out_specs = (P(AXES, None), P(AXES, None))
    return jax.shard_map(body, mesh=mesh, in_specs=in_specs, out_specs=out_specs, check_vma=False)
```

```python
import functools

import jax
import jax.numpy as jnp
from jax import lax
from jax.experimental import pallas as pl
from jax.experimental.pallas import tpu as pltpu
from jax.sharding import PartitionSpec as P

AXES = ("row", "col")
F32, BF16, I16, I32 = jnp.float32, jnp.bfloat16, jnp.int16, jnp.int32
BS = 128
EXTRA = 8
LOG_TOP = 14.997
STEPS = 64.0
LEAST = 1e-30
FINE = 65000.0

ANY = pl.BlockSpec(memory_space=pl.ANY)
SMEM = pl.BlockSpec(memory_space=pltpu.SMEM)
VMEM = pl.BlockSpec(memory_space=pltpu.VMEM)
HBM = pl.BlockSpec(memory_space=pltpu.HBM)


def params(mib):
    return pltpu.CompilerParams(vmem_limit_bytes=mib << 20)


def held(x):
    return pltpu.with_memory_space_constraint(x, pltpu.HBM)


def swap(x):
    cores = lax.axis_size("col")
    return lax.ppermute(x, "col", [(k, k ^ 1) for k in range(cores)])


def exchange(x):
    return lax.all_to_all(x, AXES, split_axis=0, concat_axis=0, tiled=True)


def fetch(hbm, vmem, sems, chunk):
    return [
        pltpu.make_async_copy(
            hbm.at[pl.ds(c * chunk, chunk)], vmem.at[pl.ds(c * chunk, chunk)], sems.at[c]
        )
        for c in range(hbm.shape[0] // chunk)
    ]


def run_chunks(copies, group):
    def step(c, _):
        for k, copy in enumerate(copies):

            @pl.when(c == k)
            def _():
                copy.wait()

        group(c)
        return 0

    lax.fori_loop(0, len(copies), step, 0)


def histogram(seeds_ref, out_ref, factor):
    columns, depth = seeds_ref.shape
    blocks = out_ref.shape[0] // columns
    unroll = 8
    none = jnp.zeros((blocks, depth), BF16)

    def group(g, _):
        for u in range(unroll):
            s = (g * unroll + u) * 2
            highs, lows = [], []
            for one in range(2):
                local = seeds_ref[pl.ds(s + one, 1), :] & (blocks * BS - 1)
                highs.append((lax.broadcasted_iota(I32, (blocks, depth), 0) == (local >> 7)).astype(F32).astype(BF16))
                lows.append((lax.broadcasted_iota(I32, (BS, depth), 0) == (local & (BS - 1))).astype(F32).astype(BF16))
            left = jnp.concatenate(
                [jnp.concatenate([highs[0], none], axis=1), jnp.concatenate([none, highs[1]], axis=1)], axis=0
            )
            count = lax.dot_general(
                left, jnp.concatenate(lows, axis=1), (((1,), (1,)), ((), ())), preferred_element_type=F32
            )
            for one in range(2):
                out_ref[pl.ds(s + one, blocks, stride=columns), :] = count[one * blocks : (one + 1) * blocks] * factor
        return 0

    lax.fori_loop(0, columns // (2 * unroll), group, 0)


def encode_scale(largest):
    return jnp.ceil(jnp.log2(jnp.maximum(largest, LEAST)) * STEPS)


def up(code):
    return jnp.exp2(LOG_TOP - code * (1.0 / STEPS))


def down(code):
    return jnp.exp2(code * (1.0 / STEPS) - LOG_TOP)


def to_i16(x):
    return jnp.round(x).astype(I32).astype(I16)


def push(x_ref, tiles, copies, src, slot, acc):
    def clear(g, _):
        acc[g] = jnp.zeros(acc.shape[1:], F32)
        return 0

    lax.fori_loop(0, acc.shape[0], clear, 0, unroll=4)
    unroll = tiles.shape[0] // len(copies)

    def group(g):
        base = g * unroll
        parts = [
            jnp.dot(x_ref[src[base + u]], tiles[base + u], preferred_element_type=F32)
            for u in range(unroll)
        ]
        for u in range(unroll):
            at = slot[base + u]
            acc[at] = acc[at] + parts[u]

    run_chunks(copies, group)


def send(acc, extra_row, staged, out_hbm, sems, chunk, lists=None):
    copies = []
    row = lax.broadcasted_iota(I32, (EXTRA, BS), 0)
    unroll = min(8, chunk)
    for c in range(acc.shape[0] // chunk):

        def group(g, _):
            for u in range(unroll):
                p = c * chunk + g * unroll + u
                block = acc[p]
                code = encode_scale(jnp.max(jnp.abs(block), axis=0, keepdims=True))
                staged[p, 0:BS, :] = to_i16(block * up(code))
                tail = jnp.where(row == 0, jnp.broadcast_to(code.astype(I32), (EXTRA, BS)), extra_row(p))
                staged[p, BS : BS + EXTRA, :] = tail.astype(I16)
                if lists is not None:
                    staged[p, BS + EXTRA :, :] = lists[u % 2]
            return 0

        lax.fori_loop(0, chunk // unroll, group, 0)
        copy = pltpu.make_async_copy(
            staged.at[pl.ds(c * chunk, chunk)], out_hbm.at[pl.ds(c * chunk, chunk)], sems.at[c]
        )
        copy.start()
        copies.append(copy)
    for copy in copies:
        copy.wait()


def receive(arrived, copies, ids, total, chunk, also=None):
    for b in range(total.shape[0]):
        total[b] = jnp.zeros(total.shape[1:], F32)
    unroll = min(16, chunk)
    for c, copy in enumerate(copies):
        if copy is not None:
            copy.wait()
        at_chunk = ids(c)

        def group(g, _):
            for u in range(unroll):
                one = g * unroll + u
                p = c * chunk + one
                tail = arrived[p, BS : BS + EXTRA, :].astype(I32).astype(F32)
                values = arrived[p, 0:BS, :].astype(I32).astype(F32) * down(tail[0:1])
                at = at_chunk(one)
                total[at] = total[at] + values
                if also is not None:
                    also(at, tail)
            return 0

        lax.fori_loop(0, chunk // unroll, group, 0)


def ids_in(ids):
    return lambda c: lambda one: ids[c, 0, one]


def first_kernel(slots_chunk, tiles_chunk, factor, src, slot, slot_block, seeds, spam_turned, degree, tiles_hbm,
                 out_hbm, good, x, tiles, counts, acc, staged, tile_sems, out_sems):
    copies = fetch(tiles_hbm, tiles, tile_sems, tiles_chunk)
    for copy in copies:
        copy.start()
    histogram(seeds, counts, factor)
    blocks, columns = x.shape[0], x.shape[1]

    def scale(b, _):
        trust = counts[pl.ds(b * columns, columns), :]
        good[b] = trust.astype(BF16)
        x[b] = (trust / degree[b].astype(F32)).astype(BF16)
        return 0

    lax.fori_loop(0, blocks, scale, 0, unroll=4)
    push(x, tiles, copies, src, slot, acc)
    local = (spam_turned[...] & (blocks * BS - 1)).astype(I16)
    half = local.shape[0] // 2
    lists = (local[0:half], local[half:])
    send(acc, lambda p: slot_block[p], staged, out_hbm, out_sems, slots_chunk, lists)


def second_kernel(slots_chunk, tiles_chunk, src, slot, degree, good, weights, arrived_hbm, tiles_hbm, out_hbm, ids_out,
                  arrived, tiles, x, total, acc, staged, ids, in_sems, tile_sems, id_sems, out_sems):
    incoming = fetch(arrived_hbm, arrived, in_sems, slots_chunk)
    copies = fetch(tiles_hbm, tiles, tile_sems, tiles_chunk)
    for copy in incoming + copies:
        copy.start()
    lane = lax.broadcasted_iota(I32, (1, BS), 1)
    moves = []

    def collect(c):
        incoming[c].wait()
        row = jnp.zeros((1, BS), I32)
        for u in range(slots_chunk):
            tail = arrived[c * slots_chunk + u, BS : BS + EXTRA, :].astype(I32)
            row = jnp.where(lane == u, tail[1:2], row)
        ids_out[c] = row
        move = pltpu.make_async_copy(ids_out.at[c], ids.at[c], id_sems.at[c])
        move.start()
        moves.append(move)

    chunks = len(incoming)
    for c in range(min(2, chunks)):
        collect(c)

    def ids_of(c):
        if c + 2 < chunks:
            collect(c + 2)
        moves[c].wait()
        return lambda one: ids[c, 0, one]

    receive(arrived, [None] * chunks, ids_of, total, slots_chunk)

    def scale(b, _):
        trust = 0.85 * total[b] + 0.15 * good[b].astype(F32)
        x[b] = (trust / degree[b].astype(F32)).astype(BF16)
        return 0

    lax.fori_loop(0, x.shape[0], scale, 0, unroll=4)
    push(x, tiles, copies, src, slot, acc)
    send(acc, lambda p: weights[p].astype(I32), staged, out_hbm, out_sems, slots_chunk)


def requests(share, ids, staged, out_hbm, sems, chunk):
    copies = []
    unroll = min(16, chunk)
    for c in range(staged.shape[0] // chunk):

        def group(g, _):
            for u in range(unroll):
                one = g * unroll + u
                staged[c * chunk + one] = share[ids[c, 0, one]]
            return 0

        lax.fori_loop(0, chunk // unroll, group, 0)
        copy = pltpu.make_async_copy(
            staged.at[pl.ds(c * chunk, chunk)], out_hbm.at[pl.ds(c * chunk, chunk)], sems.at[c]
        )
        copy.start()
        copies.append(copy)
    for copy in copies:
        copy.wait()


def third_kernel(slots_chunk, ids, good, spam, spam_hosts, arrived_hbm, out_hbm, trust, shield, in_weight,
                 arrived, total, share, staged, in_sems, out_sem):
    incoming = fetch(arrived_hbm, arrived, in_sems, slots_chunk)
    for copy in incoming:
        copy.start()
    blocks, columns = total.shape[0], total.shape[1]
    in_weight[...] = jnp.ones(in_weight.shape, F32)

    def add_weight(at, tail):
        value = (tail[2:3] + tail[3:4] * (1.0 / FINE)) * down(tail[1:2])
        in_weight[at] = in_weight[at] + value

    receive(arrived, incoming, ids_in(ids), total, slots_chunk, add_weight)
    local = spam_hosts[...] & (blocks * BS - 1)
    low, high = local & (BS - 1), local >> 7
    half = columns // 2
    left = lax.broadcasted_iota(I32, low.shape, 1) < BS // 2

    def finish(b, listed):
        value = 0.85 * total[b] + 0.15 * good[b].astype(F32)
        trust[b] = value
        keep = 1.0 / (1.0 + value)
        shield[b] = keep
        part = keep * spam[b].astype(F32) / in_weight[b]
        found = [
            jnp.take_along_axis(p, low, axis=1, mode="promise_in_bounds") for p in (part[0:half], part[half:])
        ]
        return jnp.where(high == b, jnp.where(left, found[0], found[1]), listed)

    listed = lax.fori_loop(0, blocks, finish, jnp.zeros(low.shape, F32), unroll=4)
    share[...] = listed.astype(BF16)
    rows = half // 2
    parts = (share[0:rows], share[rows:])
    for p in range(staged.shape[0]):
        staged[p] = parts[p % 2]
    copy = pltpu.make_async_copy(staged, out_hbm, out_sem)
    copy.start()
    copy.wait()


def two_halves(core, mine_hbm, other_hbm, whole, sems, rows):
    return [
        pltpu.make_async_copy(
            half, whole.at[:, pl.ds(pl.multiple_of(place * rows, rows), rows)], sems.at[n]
        )
        for n, (half, place) in enumerate(((mine_hbm, core[0]), (other_hbm, 1 - core[0])))
    ]


def places_kernel(core, slot_block, mine_hbm, other_hbm, out_hbm, lists, staged, sems, out_sem):
    columns = staged.shape[1]
    depth = lists.shape[1]
    copies = two_halves(core, mine_hbm, other_hbm, lists, sems, depth // 2)
    for copy in copies:
        copy.start()
    for copy in copies:
        copy.wait()
    host = lax.broadcasted_iota(I32, (BS, columns), 0).astype(F32).astype(BF16)
    lower = lax.broadcasted_iota(I32, (columns, BS), 0) >= columns // 2

    def one(q, _):
        offset = lists[q].astype(I32) - slot_block[q] * BS
        offset = offset.astype(F32).astype(BF16)
        at = jnp.full((BS, columns), -1.0, BF16)
        for j in range(depth):
            at = jnp.where(offset[j : j + 1] == host, jnp.array(j, BF16), at)
        place = jnp.transpose(at.astype(F32))
        place = jnp.where(lower & (place >= 0.0), place + float(depth), place)
        staged[q] = place.astype(I32).astype(I16)
        return 0

    lax.fori_loop(0, staged.shape[0], one, 0)
    back = pltpu.make_async_copy(staged, out_hbm, out_sem)
    back.start()
    back.wait()


def pack_kernel(pairs, tiles_hbm, out_hbm, tiles, staged, sem, out_sem):
    copy = pltpu.make_async_copy(tiles_hbm, tiles, sem)
    copy.start()
    copy.wait()
    size = tiles.shape[1]

    def turn(k, _):
        staged[k, 0:size, :] = jnp.transpose(tiles[pairs[1, k]])
        staged[k, size : 2 * size, :] = jnp.transpose(tiles[pairs[2, k]])
        return 0

    lax.fori_loop(0, staged.shape[0], turn, 0)
    back = pltpu.make_async_copy(staged, out_hbm, out_sem)
    back.start()
    back.wait()


def pull(pairs, y, packed, copies, total):
    y[y.shape[0] - 1] = jnp.zeros(y.shape[1:], BF16)
    for b in range(total.shape[0]):
        total[b] = jnp.zeros(total.shape[1:], F32)
    unroll = packed.shape[0] // len(copies)

    def group(g):
        parts = []
        for u in range(unroll):
            k = g * unroll + u
            left = jnp.concatenate([y[pairs[3, k]], y[pairs[4, k]]], axis=1)
            parts.append(jnp.dot(left, packed[k], preferred_element_type=F32))
        for u in range(unroll):
            at = pairs[0, g * unroll + u]
            total[at] = total[at] + parts[u]

    run_chunks(copies, group)


def fourth_kernel(slots_chunk, core, ids, pairs, spam, shield, in_weight, mine_hbm, other_hbm, places_hbm, packed_hbm,
                  out_hbm, values, places, y, packed, total, share, staged, half_sems, in_sems, pair_sems, out_sems):
    halves = two_halves(core, mine_hbm, other_hbm, values, half_sems, values.shape[1] // 2)
    incoming = fetch(places_hbm, places, in_sems, slots_chunk)
    copies = fetch(packed_hbm, packed, pair_sems, packed.shape[0] // pair_sems.shape[0])
    for copy in halves + incoming:
        copy.start(priority=0)
    for copy in copies:
        copy.start(priority=1)
    for copy in halves:
        copy.wait()
    unroll = min(8, slots_chunk)
    rows = values.shape[1]

    def expand(c):
        def group(g, _):
            for u in range(unroll):
                q = c * slots_chunk + g * unroll + u
                value = values[q].astype(F32)
                for h in range(2):
                    place = places[q, h * rows : (h + 1) * rows, :].astype(I32)
                    found = jnp.take_along_axis(value, jnp.maximum(place, 0), axis=1, mode="promise_in_bounds")
                    y[q, h * rows : (h + 1) * rows, :] = jnp.where(place >= 0, found, 0.0).astype(BF16)
            return 0

        lax.fori_loop(0, slots_chunk // unroll, group, 0)

    run_chunks(incoming, expand)
    pull(pairs, y, packed, copies, total)

    def finish(b, _):
        value = 0.85 * total[b] + 0.15 * spam[b].astype(F32)
        share[b] = (shield[b] * value / in_weight[b]).astype(BF16)
        return 0

    lax.fori_loop(0, share.shape[0], finish, 0, unroll=4)
    requests(share, ids, staged, out_hbm, out_sems, slots_chunk)


def fifth_kernel(slots_chunk, pairs, spam, arrived_hbm, packed_hbm, distrust, y, packed, total, in_sems, pair_sems):
    incoming = fetch(arrived_hbm, y, in_sems, slots_chunk)
    copies = fetch(packed_hbm, packed, pair_sems, packed.shape[0] // pair_sems.shape[0])
    for copy in incoming:
        copy.start(priority=0)
    for copy in copies:
        copy.start(priority=1)
    for copy in incoming:
        copy.wait()
    pull(pairs, y, packed, copies, total)

    def finish(b, _):
        distrust[b] = jnp.transpose(0.85 * total[b] + 0.15 * spam[b].astype(F32))
        return 0

    lax.fori_loop(0, total.shape[0], finish, 0, unroll=4)


def turn_kernel(wide, tall):
    def turn(b, _):
        tall[b] = jnp.transpose(wide[b])
        return 0

    lax.fori_loop(0, wide.shape[0], turn, 0)


def side_kernel(factor, seeds, slot, tiles_hbm, spam, weights, tiles, counts, sums, sem):
    copy = pltpu.make_async_copy(tiles_hbm, tiles, sem)
    copy.start()
    histogram(seeds, counts, factor)
    blocks, columns = spam.shape[0], spam.shape[1]

    def keep(b, _):
        spam[b] = counts[pl.ds(b * columns, columns), :].astype(BF16)
        return 0

    lax.fori_loop(0, blocks, keep, 0)
    copy.wait()
    sums[...] = jnp.zeros(sums.shape, F32)
    unroll = 4

    def group(g, _):
        for u in range(unroll):
            k = g * unroll + u
            at = slot[k]
            sums[at] = sums[at] + jnp.sum(tiles[k].astype(F32), axis=0, keepdims=True)
        return 0

    lax.fori_loop(0, tiles.shape[0] // unroll, group, 0)
    row = lax.broadcasted_iota(I32, (EXTRA, BS), 0)

    def pack(p, _):
        value = sums[p]
        code = encode_scale(jnp.abs(value))
        whole = value * up(code)
        coarse = jnp.round(whole)
        fine = jnp.round((whole - coarse) * FINE)
        wide = lambda v: jnp.broadcast_to(v, (EXTRA, BS)).astype(I32)
        tail = jnp.where(row == 1, wide(code), jnp.where(row == 2, wide(coarse), jnp.where(row == 3, wide(fine), 0)))
        weights[p] = tail.astype(I16)
        return 0

    lax.fori_loop(0, sums.shape[0], pack, 0)


def cost(flops, bytes_moved):
    return pl.CostEstimate(flops=flops, bytes_accessed=bytes_moved, transcendentals=0)


def pair_up(tile_src, tile_slot, blocks, slots):
    count = tile_src.shape[0]
    pairs = (count + blocks) // 2
    k = jnp.arange(count, dtype=I32)
    same = tile_src[:, None] == tile_src[None, :]
    rank = jnp.sum((same & (k[None, :] < k[:, None])).astype(I32), axis=1)
    block = jnp.arange(blocks, dtype=I32)
    held = jnp.sum((tile_src[:, None] == block[None, :]).astype(I32), axis=0)
    halves = (held + 1) // 2
    first = jnp.sum(jnp.where(block[:, None] < block[None, :], halves[:, None], 0), axis=0)
    start = jnp.sum(jnp.where(tile_src[:, None] == block[None, :], first[None, :], 0), axis=1)
    place = start + rank // 2
    here = place[None, :] == jnp.arange(pairs, dtype=I32)[:, None]
    even = here & (rank % 2 == 0)[None, :]
    odd = here & (rank % 2 == 1)[None, :]
    pick = lambda mask, v: jnp.sum(jnp.where(mask, v[None, :], 0), axis=1)
    shifted = tile_slot - slots
    return jnp.stack(
        [pick(even, tile_src), pick(even, k), pick(odd, k), slots + pick(even, shifted), slots + pick(odd, shifted)]
    )


def cost(flops, bytes_moved):
    return pl.CostEstimate(flops=flops, bytes_accessed=bytes_moved, transcendentals=0)


def body(tiles, tile_src, tile_slot, slot_block, out_degree, good_seeds, spam_cores):
    count, size = tiles.shape[0], tiles.shape[1]
    hosts = out_degree.shape[0]
    blocks = hosts // size
    columns = good_seeds.shape[0]
    slots = slot_block.shape[0]
    slots_chunk = min(16, slots)
    chunks = slots // slots_chunk
    sems = pltpu.SemaphoreType.DMA((chunks,))
    sds = jax.ShapeDtypeStruct
    sent = pltpu.HBM((slots, columns + EXTRA, size), I16)
    asked = pltpu.HBM((slots, columns, size), BF16)
    ids_shape = sds((chunks, 1, size), I32)
    panel = (blocks, columns, size)
    sent_buf = pltpu.VMEM(sent.shape, I16)
    asked_buf = pltpu.VMEM(asked.shape, BF16)
    y_buf = pltpu.VMEM((slots + 1, columns, size), BF16)
    total_buf = pltpu.VMEM(panel, F32)
    half_buf = pltpu.VMEM(panel, BF16)
    acc_buf = pltpu.VMEM((slots, columns, size), F32)
    counts_buf = pltpu.VMEM((blocks * columns, size), F32)
    degree = out_degree.reshape(blocks, 1, size)
    work = 2 * count * size * size * columns
    tile_bytes = 2 * count * size * size
    tiles_chunk = min(128, count)
    tiles_buf = pltpu.VMEM(tiles.shape, BF16)
    tile_sems = pltpu.SemaphoreType.DMA((count // tiles_chunk,))
    couples = (count + blocks) // 2
    pair_sems = pltpu.SemaphoreType.DMA((next(n for n in (4, 5, 2, 1) if couples % n == 0),))
    packed_shape = (couples, 2 * size, size)
    packed_buf = pltpu.VMEM(packed_shape, BF16)

    depth = spam_cores.shape[1]
    half = depth // 2
    first_sent = (slots, columns + EXTRA + half, size)
    outgoing, good = pl.pallas_call(
        functools.partial(first_kernel, slots_chunk, tiles_chunk, float(hosts / good_seeds.shape[1])),
        out_shape=(pltpu.HBM(first_sent, I16), sds(panel, BF16)),
        in_specs=[SMEM, SMEM, SMEM, VMEM, VMEM, VMEM, ANY],
        out_specs=(HBM, VMEM),
        scratch_shapes=[half_buf, tiles_buf, counts_buf, acc_buf, pltpu.VMEM(first_sent, I16), tile_sems, sems],
        compiler_params=params(57),
        cost_estimate=cost(work, 2 * tile_bytes),
        name="first_push",
    )(tile_src, tile_slot, slot_block, good_seeds, spam_cores.T, degree, held(tiles))
    arrived = exchange(outgoing)
    spam_seeds, src_after, slot_after, _ = lax.optimization_barrier((spam_cores, tile_src, tile_slot, outgoing))
    spam_hosts = jnp.concatenate([spam_seeds[: columns // 2], spam_seeds[columns // 2 :]], axis=1)
    spam, weights = pl.pallas_call(
        functools.partial(side_kernel, float(hosts / spam_cores.shape[1])),
        out_shape=(sds(panel, BF16), sds((slots, EXTRA, size), I16)),
        in_specs=[VMEM, SMEM, ANY],
        out_specs=(VMEM, VMEM),
        scratch_shapes=[tiles_buf, counts_buf, pltpu.VMEM((slots, 1, size), F32), pltpu.SemaphoreType.DMA],
        compiler_params=params(40),
        cost_estimate=cost(work // 4, tile_bytes),
        name="side",
    )(spam_seeds, slot_after, held(tiles))
    pairs = pair_up(src_after, slot_after, blocks, slots)
    pair_tiles = lax.optimization_barrier((pairs, outgoing))[0]
    packed = pl.pallas_call(
        pack_kernel,
        out_shape=pltpu.HBM(packed_shape, BF16),
        in_specs=[SMEM, ANY],
        out_specs=HBM,
        scratch_shapes=[tiles_buf, packed_buf, pltpu.SemaphoreType.DMA, pltpu.SemaphoreType.DMA],
        compiler_params=params(40),
        cost_estimate=cost(work // 4, 2 * tile_bytes),
        name="pack",
    )(pair_tiles, held(tiles))
    arrived, packed, weights = lax.optimization_barrier((arrived, packed, weights))
    outgoing, ids = pl.pallas_call(
        functools.partial(second_kernel, slots_chunk, tiles_chunk),
        out_shape=(sent, ids_shape),
        in_specs=[SMEM, SMEM, VMEM, VMEM, VMEM, HBM, ANY],
        out_specs=(HBM, VMEM),
        scratch_shapes=[
            pltpu.VMEM(first_sent, I16), tiles_buf, half_buf, total_buf, acc_buf, sent_buf,
            pltpu.SMEM(ids_shape.shape, I32), sems, tile_sems, sems, sems,
        ],
        compiler_params=params(40),
        cost_estimate=cost(work, 2 * tile_bytes),
        name="second_push",
    )(tile_src, tile_slot, degree, good, weights, held(arrived), held(tiles))
    first_arrived, _ = lax.optimization_barrier((arrived, outgoing))
    arrived = exchange(outgoing)
    core = (lax.axis_index("col") % 2).astype(I32)[None]
    mine = first_arrived[:, columns + EXTRA :, :]
    places = pl.pallas_call(
        places_kernel,
        out_shape=pltpu.HBM((slots, columns, size), I16),
        in_specs=[SMEM, SMEM, ANY, ANY],
        out_specs=HBM,
        scratch_shapes=[
            pltpu.VMEM((slots, depth, size), I16), pltpu.VMEM((slots, columns, size), I16),
            pltpu.SemaphoreType.DMA((2,)), pltpu.SemaphoreType.DMA,
        ],
        compiler_params=params(40),
        cost_estimate=cost(work, tile_bytes),
        name="places",
    )(core, slot_block, mine, swap(mine))
    arrived, places = lax.optimization_barrier((arrived, places))
    listed_shape = (slots, columns // 4, size)
    outgoing, trust, shield, in_weight = pl.pallas_call(
        functools.partial(third_kernel, slots_chunk),
        out_shape=(pltpu.HBM(listed_shape, BF16), sds(panel, F32), sds(panel, F32), sds((blocks, 1, size), F32)),
        in_specs=[SMEM, VMEM, VMEM, VMEM, HBM],
        out_specs=(HBM, VMEM, VMEM, VMEM),
        scratch_shapes=[
            sent_buf, total_buf, pltpu.VMEM((columns // 2, size), BF16), pltpu.VMEM(listed_shape, BF16),
            sems, pltpu.SemaphoreType.DMA,
        ],
        compiler_params=params(40),
        cost_estimate=cost(work // 8, tile_bytes),
        name="first_shares",
    )(ids, good, spam, spam_hosts, held(arrived))
    mine = exchange(outgoing)
    trust_out = pl.pallas_call(
        turn_kernel,
        out_shape=sds((blocks, size, columns), F32),
        in_specs=[VMEM],
        out_specs=VMEM,
        compiler_params=params(16),
        cost_estimate=cost(work // 64, tile_bytes // 4),
        name="turn",
    )(trust)
    asked_for = pl.pallas_call(
        functools.partial(fourth_kernel, slots_chunk),
        out_shape=asked,
        in_specs=[SMEM, SMEM, SMEM, VMEM, VMEM, VMEM, ANY, ANY, HBM, HBM],
        out_specs=HBM,
        scratch_shapes=[
            pltpu.VMEM((slots, columns // 2, size), BF16), pltpu.VMEM((slots, columns, size), I16),
            y_buf, packed_buf, total_buf, half_buf, asked_buf, pltpu.SemaphoreType.DMA((2,)), sems, pair_sems, sems,
        ],
        compiler_params=params(44),
        cost_estimate=cost(work, 2 * tile_bytes),
        name="second_shares",
    )(core, ids, pairs, spam, shield, in_weight, mine, swap(mine), held(places), held(packed))
    arrived = exchange(asked_for)
    distrust = pl.pallas_call(
        functools.partial(fifth_kernel, slots_chunk),
        out_shape=sds((blocks, size, columns), F32),
        in_specs=[SMEM, VMEM, HBM, HBM],
        out_specs=VMEM,
        scratch_shapes=[y_buf, packed_buf, total_buf, sems, pair_sems],
        compiler_params=params(40),
        cost_estimate=cost(work, 2 * tile_bytes),
        name="last_pull",
    )(pairs, spam, held(arrived), held(packed))
    return trust_out.reshape(hosts, columns), distrust.reshape(hosts, columns)


def solution(mesh):
    in_specs = (
        P(AXES, None, None),
        P(AXES),
        P(AXES),
        P(AXES),
        P(AXES),
        P(None, AXES),
        P(None, AXES),
    )
    out_specs = (P(AXES, None), P(AXES, None))
    return jax.shard_map(body, mesh=mesh, in_specs=in_specs, out_specs=out_specs, check_vma=False)
```

```python
import functools

import jax
import jax.numpy as jnp
from jax import lax
from jax.experimental import pallas as pl
from jax.experimental.pallas import tpu as pltpu
from jax.sharding import PartitionSpec as P

AXES = ("row", "col")
F32, BF16, I16, I32 = jnp.float32, jnp.bfloat16, jnp.int16, jnp.int32
BS = 128
EXTRA = 8
LOG_TOP = 14.997
STEPS = 64.0
LEAST = 1e-30
FINE = 65000.0

ANY = pl.BlockSpec(memory_space=pl.ANY)
SMEM = pl.BlockSpec(memory_space=pltpu.SMEM)
VMEM = pl.BlockSpec(memory_space=pltpu.VMEM)
HBM = pl.BlockSpec(memory_space=pltpu.HBM)


def params(mib):
    return pltpu.CompilerParams(vmem_limit_bytes=mib << 20)


def held(x):
    return pltpu.with_memory_space_constraint(x, pltpu.HBM)


def swap(x):
    cores = lax.axis_size("col")
    return lax.ppermute(x, "col", [(k, k ^ 1) for k in range(cores)])


def exchange(x):
    return lax.all_to_all(x, AXES, split_axis=0, concat_axis=0, tiled=True)


def fetch(hbm, vmem, sems, chunk):
    return [
        pltpu.make_async_copy(
            hbm.at[pl.ds(c * chunk, chunk)], vmem.at[pl.ds(c * chunk, chunk)], sems.at[c]
        )
        for c in range(hbm.shape[0] // chunk)
    ]


def clear_all(acc):
    def clear(g, _):
        acc[g] = jnp.zeros(acc.shape[1:], F32)
        return 0

    lax.fori_loop(0, acc.shape[0], clear, 0, unroll=4)


def run_chunks(copies, group):
    def step(c, _):
        for k, copy in enumerate(copies):

            @pl.when(c == k)
            def _():
                copy.wait()

        group(c)
        return 0

    lax.fori_loop(0, len(copies), step, 0)


def histogram(seeds_ref, out_ref, factor, to_clear=None):
    columns, depth = seeds_ref.shape
    blocks = out_ref.shape[0] // columns
    unroll = 16
    none = jnp.zeros((blocks, depth), BF16)

    steps = columns // (2 * unroll)

    def group(g, _):
        if to_clear is not None:
            part = to_clear.shape[0] // steps
            for u in range(part):
                to_clear[g * part + u] = jnp.zeros(to_clear.shape[1:], F32)
        for u in range(unroll):
            s = (g * unroll + u) * 2
            highs, lows = [], []
            for one in range(2):
                local = seeds_ref[pl.ds(s + one, 1), :] & (blocks * BS - 1)
                highs.append((lax.broadcasted_iota(I32, (blocks, depth), 0) == (local >> 7)).astype(F32).astype(BF16))
                lows.append((lax.broadcasted_iota(I32, (BS, depth), 0) == (local & (BS - 1))).astype(F32).astype(BF16))
            left = jnp.concatenate(
                [jnp.concatenate([highs[0], none], axis=1), jnp.concatenate([none, highs[1]], axis=1)], axis=0
            )
            count = lax.dot_general(
                left, jnp.concatenate(lows, axis=1), (((1,), (1,)), ((), ())), preferred_element_type=F32
            )
            for one in range(2):
                out_ref[pl.ds(s + one, blocks, stride=columns), :] = count[one * blocks : (one + 1) * blocks] * factor
        return 0

    lax.fori_loop(0, steps, group, 0)


def encode_scale(largest):
    return jnp.ceil(jnp.log2(jnp.maximum(largest, LEAST)) * STEPS)


def up(code):
    return jnp.exp2(LOG_TOP - code * (1.0 / STEPS))


def down(code):
    return jnp.exp2(code * (1.0 / STEPS) - LOG_TOP)


def to_i16(x):
    return jnp.round(x).astype(I32).astype(I16)


def push(x_ref, tiles, copies, src, slot, acc):
    unroll = tiles.shape[0] // len(copies)

    def group(g):
        base = g * unroll
        parts = [
            jnp.dot(x_ref[src[base + u]], tiles[base + u], preferred_element_type=F32)
            for u in range(unroll)
        ]
        for u in range(unroll):
            at = slot[base + u]
            acc[at] = acc[at] + parts[u]

    run_chunks(copies, group)


def send(acc, extra_row, staged, out_hbm, sems, chunk, lists=None):
    copies = []
    row = lax.broadcasted_iota(I32, (EXTRA, BS), 0)
    unroll = min(8, chunk)
    for c in range(acc.shape[0] // chunk):

        def group(g, _):
            for u in range(unroll):
                p = c * chunk + g * unroll + u
                block = acc[p]
                code = encode_scale(jnp.max(jnp.abs(block), axis=0, keepdims=True))
                staged[p, 0:BS, :] = to_i16(block * up(code))
                tail = jnp.where(row == 0, jnp.broadcast_to(code.astype(I32), (EXTRA, BS)), extra_row(p))
                staged[p, BS : BS + EXTRA, :] = tail.astype(I16)
                if lists is not None:
                    staged[p, BS + EXTRA :, :] = lists[u % 2]
            return 0

        lax.fori_loop(0, chunk // unroll, group, 0)
        copy = pltpu.make_async_copy(
            staged.at[pl.ds(c * chunk, chunk)], out_hbm.at[pl.ds(c * chunk, chunk)], sems.at[c]
        )
        copy.start()
        copies.append(copy)
    for copy in copies:
        copy.wait()


def receive(arrived, copies, ids, total, chunk, also=None):
    for b in range(total.shape[0]):
        total[b] = jnp.zeros(total.shape[1:], F32)
    unroll = min(16, chunk)
    for c, copy in enumerate(copies):
        if copy is not None:
            copy.wait()
        at_chunk = ids(c)

        def group(g, _):
            for u in range(unroll):
                one = g * unroll + u
                p = c * chunk + one
                tail = arrived[p, BS : BS + EXTRA, :].astype(I32).astype(F32)
                values = arrived[p, 0:BS, :].astype(I32).astype(F32) * down(tail[0:1])
                at = at_chunk(one)
                total[at] = total[at] + values
                if also is not None:
                    also(at, tail)
            return 0

        lax.fori_loop(0, chunk // unroll, group, 0)


def ids_in(ids):
    return lambda c: lambda one: ids[c, 0, one]


def first_kernel(slots_chunk, tiles_chunk, factor, src, slot, slot_block, seeds, spam_turned, degree, tiles_hbm,
                 out_hbm, good, x, tiles, counts, acc, staged, tile_sems, out_sems):
    copies = fetch(tiles_hbm, tiles, tile_sems, tiles_chunk)
    for copy in copies:
        copy.start()
    histogram(seeds, counts, factor, acc)
    blocks, columns = x.shape[0], x.shape[1]

    def scale(b, _):
        trust = counts[pl.ds(b * columns, columns), :]
        good[b] = trust.astype(BF16)
        x[b] = (trust / degree[b].astype(F32)).astype(BF16)
        return 0

    lax.fori_loop(0, blocks, scale, 0, unroll=4)
    push(x, tiles, copies, src, slot, acc)
    local = (spam_turned[...] & (blocks * BS - 1)).astype(I16)
    half = local.shape[0] // 2
    lists = (local[0:half], local[half:])
    send(acc, lambda p: slot_block[p], staged, out_hbm, out_sems, slots_chunk, lists)


def second_kernel(slots_chunk, tiles_chunk, src, slot, degree, good, weights, arrived_hbm, tiles_hbm, out_hbm, ids_out,
                  arrived, tiles, x, total, acc, staged, ids, in_sems, tile_sems, id_sems, out_sems):
    incoming = fetch(arrived_hbm, arrived, in_sems, slots_chunk)
    copies = fetch(tiles_hbm, tiles, tile_sems, tiles_chunk)
    for copy in incoming:
        copy.start(priority=0)
    for copy in copies:
        copy.start(priority=1)
    clear_all(acc)
    lane = lax.broadcasted_iota(I32, (1, BS), 1)
    moves = []

    def collect(c):
        incoming[c].wait()
        row = jnp.zeros((1, BS), I32)
        for u in range(slots_chunk):
            tail = arrived[c * slots_chunk + u, BS : BS + EXTRA, :].astype(I32)
            row = jnp.where(lane == u, tail[1:2], row)
        ids_out[c] = row
        move = pltpu.make_async_copy(ids_out.at[c], ids.at[c], id_sems.at[c])
        move.start()
        moves.append(move)

    chunks = len(incoming)
    for c in range(min(2, chunks)):
        collect(c)

    def ids_of(c):
        if c + 2 < chunks:
            collect(c + 2)
        moves[c].wait()
        return lambda one: ids[c, 0, one]

    receive(arrived, [None] * chunks, ids_of, total, slots_chunk)

    def scale(b, _):
        trust = 0.85 * total[b] + 0.15 * good[b].astype(F32)
        x[b] = (trust / degree[b].astype(F32)).astype(BF16)
        return 0

    lax.fori_loop(0, x.shape[0], scale, 0, unroll=4)
    push(x, tiles, copies, src, slot, acc)
    send(acc, lambda p: weights[p].astype(I32), staged, out_hbm, out_sems, slots_chunk)


def requests(share, ids, staged, out_hbm, sems, chunk):
    copies = []
    unroll = min(16, chunk)
    for c in range(staged.shape[0] // chunk):

        def group(g, _):
            for u in range(unroll):
                one = g * unroll + u
                staged[c * chunk + one] = share[ids[c, 0, one]]
            return 0

        lax.fori_loop(0, chunk // unroll, group, 0)
        copy = pltpu.make_async_copy(
            staged.at[pl.ds(c * chunk, chunk)], out_hbm.at[pl.ds(c * chunk, chunk)], sems.at[c]
        )
        copy.start()
        copies.append(copy)
    for copy in copies:
        copy.wait()


def third_kernel(slots_chunk, ids, good, spam, spam_hosts, arrived_hbm, out_hbm, trust, shield, in_weight,
                 arrived, total, share, staged, in_sems, out_sem):
    incoming = fetch(arrived_hbm, arrived, in_sems, slots_chunk)
    for copy in incoming:
        copy.start()
    blocks, columns = total.shape[0], total.shape[1]
    in_weight[...] = jnp.ones(in_weight.shape, F32)

    def add_weight(at, tail):
        value = (tail[2:3] + tail[3:4] * (1.0 / FINE)) * down(tail[1:2])
        in_weight[at] = in_weight[at] + value

    receive(arrived, incoming, ids_in(ids), total, slots_chunk, add_weight)
    local = spam_hosts[...] & (blocks * BS - 1)
    low, high = local & (BS - 1), local >> 7
    half = columns // 2
    left = lax.broadcasted_iota(I32, low.shape, 1) < BS // 2

    def finish(b, listed):
        value = 0.85 * total[b] + 0.15 * good[b].astype(F32)
        trust[b] = value
        keep = 1.0 / (1.0 + value)
        shield[b] = keep
        part = keep * spam[b].astype(F32) / in_weight[b]
        found = [
            jnp.take_along_axis(p, low, axis=1, mode="promise_in_bounds") for p in (part[0:half], part[half:])
        ]
        return jnp.where(high == b, jnp.where(left, found[0], found[1]), listed)

    listed = lax.fori_loop(0, blocks, finish, jnp.zeros(low.shape, F32), unroll=4)
    share[...] = listed.astype(BF16)
    rows = half // 2
    parts = (share[0:rows], share[rows:])
    for p in range(staged.shape[0]):
        staged[p] = parts[p % 2]
    copy = pltpu.make_async_copy(staged, out_hbm, out_sem)
    copy.start()
    copy.wait()


def two_halves(core, mine_hbm, other_hbm, whole, sems, rows):
    return [
        pltpu.make_async_copy(
            half, whole.at[:, pl.ds(pl.multiple_of(place * rows, rows), rows)], sems.at[n]
        )
        for n, (half, place) in enumerate(((mine_hbm, core[0]), (other_hbm, 1 - core[0])))
    ]


def places_kernel(core, slot_block, mine_hbm, other_hbm, out_hbm, lists, staged, sems, out_sem):
    columns = staged.shape[1]
    depth = lists.shape[1]
    copies = two_halves(core, mine_hbm, other_hbm, lists, sems, depth // 2)
    for copy in copies:
        copy.start()
    for copy in copies:
        copy.wait()
    host = lax.broadcasted_iota(I32, (BS, columns), 0).astype(F32).astype(BF16)
    lower = lax.broadcasted_iota(I32, (columns, BS), 0) >= columns // 2

    def one(q, _):
        offset = lists[q].astype(I32) - slot_block[q] * BS
        offset = offset.astype(F32).astype(BF16)
        at = jnp.full((BS, columns), -1.0, BF16)
        for j in range(depth):
            at = jnp.where(offset[j : j + 1] == host, jnp.array(j, BF16), at)
        place = jnp.transpose(at.astype(F32))
        place = jnp.where(lower & (place >= 0.0), place + float(depth), place)
        staged[q] = place.astype(I32).astype(I16)
        return 0

    lax.fori_loop(0, staged.shape[0], one, 0)
    back = pltpu.make_async_copy(staged, out_hbm, out_sem)
    back.start()
    back.wait()


def pack_kernel(pairs, tiles_hbm, out_hbm, tiles, staged, sem, out_sem):
    copy = pltpu.make_async_copy(tiles_hbm, tiles, sem)
    copy.start()
    copy.wait()
    size = tiles.shape[1]

    def turn(k, _):
        staged[k, 0:size, :] = jnp.transpose(tiles[pairs[1, k]])
        staged[k, size : 2 * size, :] = jnp.transpose(tiles[pairs[2, k]])
        return 0

    lax.fori_loop(0, staged.shape[0], turn, 0)
    back = pltpu.make_async_copy(staged, out_hbm, out_sem)
    back.start()
    back.wait()


def before_pull(y, total):
    y[y.shape[0] - 1] = jnp.zeros(y.shape[1:], BF16)
    clear_all(total)


def pull(pairs, y, packed, copies, total):
    unroll = packed.shape[0] // len(copies)

    def group(g):
        parts = []
        for u in range(unroll):
            k = g * unroll + u
            left = jnp.concatenate([y[pairs[3, k]], y[pairs[4, k]]], axis=1)
            parts.append(jnp.dot(left, packed[k], preferred_element_type=F32))
        for u in range(unroll):
            at = pairs[0, g * unroll + u]
            total[at] = total[at] + parts[u]

    run_chunks(copies, group)


def fourth_kernel(slots_chunk, core, ids, pairs, spam, shield, in_weight, mine_hbm, other_hbm, places_hbm, packed_hbm,
                  out_hbm, values, places, y, packed, total, share, staged, half_sems, in_sems, pair_sems, out_sems):
    halves = two_halves(core, mine_hbm, other_hbm, values, half_sems, values.shape[1] // 2)
    incoming = fetch(places_hbm, places, in_sems, slots_chunk)
    copies = fetch(packed_hbm, packed, pair_sems, packed.shape[0] // pair_sems.shape[0])
    for copy in halves + incoming:
        copy.start(priority=0)
    for copy in copies:
        copy.start(priority=1)
    before_pull(y, total)
    for copy in halves:
        copy.wait()
    unroll = min(16, slots_chunk)
    rows = values.shape[1]

    def expand(c):
        def group(g, _):
            for u in range(unroll):
                q = c * slots_chunk + g * unroll + u
                value = values[q].astype(F32)
                for h in range(2):
                    place = places[q, h * rows : (h + 1) * rows, :].astype(I32)
                    found = jnp.take_along_axis(value, jnp.maximum(place, 0), axis=1, mode="promise_in_bounds")
                    y[q, h * rows : (h + 1) * rows, :] = jnp.where(place >= 0, found, 0.0).astype(BF16)
            return 0

        lax.fori_loop(0, slots_chunk // unroll, group, 0)

    run_chunks(incoming, expand)
    pull(pairs, y, packed, copies, total)

    def finish(b, _):
        value = 0.85 * total[b] + 0.15 * spam[b].astype(F32)
        share[b] = (shield[b] * value / in_weight[b]).astype(BF16)
        return 0

    lax.fori_loop(0, share.shape[0], finish, 0, unroll=4)
    requests(share, ids, staged, out_hbm, out_sems, slots_chunk)


def fifth_kernel(slots_chunk, pairs, spam, arrived_hbm, packed_hbm, distrust, y, packed, total, in_sems, pair_sems):
    incoming = fetch(arrived_hbm, y, in_sems, slots_chunk)
    copies = fetch(packed_hbm, packed, pair_sems, packed.shape[0] // pair_sems.shape[0])
    for copy in incoming:
        copy.start(priority=0)
    for copy in copies:
        copy.start(priority=1)
    before_pull(y, total)
    for copy in incoming:
        copy.wait()
    pull(pairs, y, packed, copies, total)

    def finish(b, _):
        distrust[b] = jnp.transpose(0.85 * total[b] + 0.15 * spam[b].astype(F32))
        return 0

    lax.fori_loop(0, total.shape[0], finish, 0, unroll=4)


def turn_kernel(wide, tall):
    def turn(b, _):
        tall[b] = jnp.transpose(wide[b])
        return 0

    lax.fori_loop(0, wide.shape[0], turn, 0)


def side_kernel(factor, seeds, slot, tiles_hbm, spam, weights, tiles, counts, sums, sem):
    copy = pltpu.make_async_copy(tiles_hbm, tiles, sem)
    copy.start()
    histogram(seeds, counts, factor)
    blocks, columns = spam.shape[0], spam.shape[1]

    def keep(b, _):
        spam[b] = counts[pl.ds(b * columns, columns), :].astype(BF16)
        return 0

    lax.fori_loop(0, blocks, keep, 0)
    copy.wait()
    sums[...] = jnp.zeros(sums.shape, F32)
    unroll = 4

    def group(g, _):
        for u in range(unroll):
            k = g * unroll + u
            at = slot[k]
            sums[at] = sums[at] + jnp.sum(tiles[k].astype(F32), axis=0, keepdims=True)
        return 0

    lax.fori_loop(0, tiles.shape[0] // unroll, group, 0)
    row = lax.broadcasted_iota(I32, (EXTRA, BS), 0)

    def pack(p, _):
        value = sums[p]
        code = encode_scale(jnp.abs(value))
        whole = value * up(code)
        coarse = jnp.round(whole)
        fine = jnp.round((whole - coarse) * FINE)
        wide = lambda v: jnp.broadcast_to(v, (EXTRA, BS)).astype(I32)
        tail = jnp.where(row == 1, wide(code), jnp.where(row == 2, wide(coarse), jnp.where(row == 3, wide(fine), 0)))
        weights[p] = tail.astype(I16)
        return 0

    lax.fori_loop(0, sums.shape[0], pack, 0)


def cost(flops, bytes_moved):
    return pl.CostEstimate(flops=flops, bytes_accessed=bytes_moved, transcendentals=0)


def pair_up(tile_src, tile_slot, blocks, slots):
    count = tile_src.shape[0]
    pairs = (count + blocks) // 2
    k = jnp.arange(count, dtype=I32)
    same = tile_src[:, None] == tile_src[None, :]
    rank = jnp.sum((same & (k[None, :] < k[:, None])).astype(I32), axis=1)
    block = jnp.arange(blocks, dtype=I32)
    held = jnp.sum((tile_src[:, None] == block[None, :]).astype(I32), axis=0)
    halves = (held + 1) // 2
    first = jnp.sum(jnp.where(block[:, None] < block[None, :], halves[:, None], 0), axis=0)
    start = jnp.sum(jnp.where(tile_src[:, None] == block[None, :], first[None, :], 0), axis=1)
    place = start + rank // 2
    here = place[None, :] == jnp.arange(pairs, dtype=I32)[:, None]
    even = here & (rank % 2 == 0)[None, :]
    odd = here & (rank % 2 == 1)[None, :]
    pick = lambda mask, v: jnp.sum(jnp.where(mask, v[None, :], 0), axis=1)
    shifted = tile_slot - slots
    return jnp.stack(
        [pick(even, tile_src), pick(even, k), pick(odd, k), slots + pick(even, shifted), slots + pick(odd, shifted)]
    )


def cost(flops, bytes_moved):
    return pl.CostEstimate(flops=flops, bytes_accessed=bytes_moved, transcendentals=0)


def body(tiles, tile_src, tile_slot, slot_block, out_degree, good_seeds, spam_cores):
    count, size = tiles.shape[0], tiles.shape[1]
    hosts = out_degree.shape[0]
    blocks = hosts // size
    columns = good_seeds.shape[0]
    slots = slot_block.shape[0]
    slots_chunk = min(16, slots)
    chunks = slots // slots_chunk
    sems = pltpu.SemaphoreType.DMA((chunks,))
    sds = jax.ShapeDtypeStruct
    sent = pltpu.HBM((slots, columns + EXTRA, size), I16)
    asked = pltpu.HBM((slots, columns, size), BF16)
    ids_shape = sds((chunks, 1, size), I32)
    panel = (blocks, columns, size)
    sent_buf = pltpu.VMEM(sent.shape, I16)
    asked_buf = pltpu.VMEM(asked.shape, BF16)
    y_buf = pltpu.VMEM((slots + 1, columns, size), BF16)
    total_buf = pltpu.VMEM(panel, F32)
    half_buf = pltpu.VMEM(panel, BF16)
    acc_buf = pltpu.VMEM((slots, columns, size), F32)
    counts_buf = pltpu.VMEM((blocks * columns, size), F32)
    degree = out_degree.reshape(blocks, 1, size)
    work = 2 * count * size * size * columns
    tile_bytes = 2 * count * size * size
    tiles_chunk = min(128, count)
    tiles_buf = pltpu.VMEM(tiles.shape, BF16)
    tile_sems = pltpu.SemaphoreType.DMA((count // tiles_chunk,))
    couples = (count + blocks) // 2
    pair_sems = pltpu.SemaphoreType.DMA((next(n for n in (4, 5, 2, 1) if couples % n == 0),))
    packed_shape = (couples, 2 * size, size)
    packed_buf = pltpu.VMEM(packed_shape, BF16)

    depth = spam_cores.shape[1]
    half = depth // 2
    first_sent = (slots, columns + EXTRA + half, size)
    outgoing, good = pl.pallas_call(
        functools.partial(first_kernel, slots_chunk, tiles_chunk, float(hosts / good_seeds.shape[1])),
        out_shape=(pltpu.HBM(first_sent, I16), sds(panel, BF16)),
        in_specs=[SMEM, SMEM, SMEM, VMEM, VMEM, VMEM, ANY],
        out_specs=(HBM, VMEM),
        scratch_shapes=[half_buf, tiles_buf, counts_buf, acc_buf, pltpu.VMEM(first_sent, I16), tile_sems, sems],
        compiler_params=params(57),
        cost_estimate=cost(work, 2 * tile_bytes),
        name="first_push",
    )(tile_src, tile_slot, slot_block, good_seeds, spam_cores.T, degree, held(tiles))
    arrived = exchange(outgoing)
    spam_seeds, src_after, slot_after, _ = lax.optimization_barrier((spam_cores, tile_src, tile_slot, outgoing))
    spam_hosts = jnp.concatenate([spam_seeds[: columns // 2], spam_seeds[columns // 2 :]], axis=1)
    spam, weights = pl.pallas_call(
        functools.partial(side_kernel, float(hosts / spam_cores.shape[1])),
        out_shape=(sds(panel, BF16), sds((slots, EXTRA, size), I16)),
        in_specs=[VMEM, SMEM, ANY],
        out_specs=(VMEM, VMEM),
        scratch_shapes=[tiles_buf, counts_buf, pltpu.VMEM((slots, 1, size), F32), pltpu.SemaphoreType.DMA],
        compiler_params=params(40),
        cost_estimate=cost(work // 4, tile_bytes),
        name="side",
    )(spam_seeds, slot_after, held(tiles))
    pairs = pair_up(src_after, slot_after, blocks, slots)
    pair_tiles = lax.optimization_barrier((pairs, outgoing))[0]
    packed = pl.pallas_call(
        pack_kernel,
        out_shape=pltpu.HBM(packed_shape, BF16),
        in_specs=[SMEM, ANY],
        out_specs=HBM,
        scratch_shapes=[tiles_buf, packed_buf, pltpu.SemaphoreType.DMA, pltpu.SemaphoreType.DMA],
        compiler_params=params(40),
        cost_estimate=cost(work // 4, 2 * tile_bytes),
        name="pack",
    )(pair_tiles, held(tiles))
    arrived, packed, weights = lax.optimization_barrier((arrived, packed, weights))
    outgoing, ids = pl.pallas_call(
        functools.partial(second_kernel, slots_chunk, tiles_chunk),
        out_shape=(sent, ids_shape),
        in_specs=[SMEM, SMEM, VMEM, VMEM, VMEM, HBM, ANY],
        out_specs=(HBM, VMEM),
        scratch_shapes=[
            pltpu.VMEM(first_sent, I16), tiles_buf, half_buf, total_buf, acc_buf, sent_buf,
            pltpu.SMEM(ids_shape.shape, I32), sems, tile_sems, sems, sems,
        ],
        compiler_params=params(40),
        cost_estimate=cost(work, 2 * tile_bytes),
        name="second_push",
    )(tile_src, tile_slot, degree, good, weights, held(arrived), held(tiles))
    first_arrived, _ = lax.optimization_barrier((arrived, outgoing))
    arrived = exchange(outgoing)
    core = (lax.axis_index("col") % 2).astype(I32)[None]
    mine = first_arrived[:, columns + EXTRA :, :]
    places = pl.pallas_call(
        places_kernel,
        out_shape=pltpu.HBM((slots, columns, size), I16),
        in_specs=[SMEM, SMEM, ANY, ANY],
        out_specs=HBM,
        scratch_shapes=[
            pltpu.VMEM((slots, depth, size), I16), pltpu.VMEM((slots, columns, size), I16),
            pltpu.SemaphoreType.DMA((2,)), pltpu.SemaphoreType.DMA,
        ],
        compiler_params=params(40),
        cost_estimate=cost(work, tile_bytes),
        name="places",
    )(core, slot_block, mine, swap(mine))
    arrived, places = lax.optimization_barrier((arrived, places))
    listed_shape = (slots, columns // 4, size)
    outgoing, trust, shield, in_weight = pl.pallas_call(
        functools.partial(third_kernel, slots_chunk),
        out_shape=(pltpu.HBM(listed_shape, BF16), sds(panel, F32), sds(panel, F32), sds((blocks, 1, size), F32)),
        in_specs=[SMEM, VMEM, VMEM, VMEM, HBM],
        out_specs=(HBM, VMEM, VMEM, VMEM),
        scratch_shapes=[
            sent_buf, total_buf, pltpu.VMEM((columns // 2, size), BF16), pltpu.VMEM(listed_shape, BF16),
            sems, pltpu.SemaphoreType.DMA,
        ],
        compiler_params=params(40),
        cost_estimate=cost(work // 8, tile_bytes),
        name="first_shares",
    )(ids, good, spam, spam_hosts, held(arrived))
    mine = exchange(outgoing)
    trust_out = pl.pallas_call(
        turn_kernel,
        out_shape=sds((blocks, size, columns), F32),
        in_specs=[VMEM],
        out_specs=VMEM,
        compiler_params=params(16),
        cost_estimate=cost(work // 64, tile_bytes // 4),
        name="turn",
    )(trust)
    asked_for = pl.pallas_call(
        functools.partial(fourth_kernel, slots_chunk),
        out_shape=asked,
        in_specs=[SMEM, SMEM, SMEM, VMEM, VMEM, VMEM, ANY, ANY, HBM, HBM],
        out_specs=HBM,
        scratch_shapes=[
            pltpu.VMEM((slots, columns // 2, size), BF16), pltpu.VMEM((slots, columns, size), I16),
            y_buf, packed_buf, total_buf, half_buf, asked_buf, pltpu.SemaphoreType.DMA((2,)), sems, pair_sems, sems,
        ],
        compiler_params=params(44),
        cost_estimate=cost(work, 2 * tile_bytes),
        name="second_shares",
    )(core, ids, pairs, spam, shield, in_weight, mine, swap(mine), held(places), held(packed))
    arrived = exchange(asked_for)
    distrust = pl.pallas_call(
        functools.partial(fifth_kernel, slots_chunk),
        out_shape=sds((blocks, size, columns), F32),
        in_specs=[SMEM, VMEM, HBM, HBM],
        out_specs=VMEM,
        scratch_shapes=[y_buf, packed_buf, total_buf, sems, pair_sems],
        compiler_params=params(40),
        cost_estimate=cost(work, 2 * tile_bytes),
        name="last_pull",
    )(pairs, spam, held(arrived), held(packed))
    return trust_out.reshape(hosts, columns), distrust.reshape(hosts, columns)


def solution(mesh):
    in_specs = (
        P(AXES, None, None),
        P(AXES),
        P(AXES),
        P(AXES),
        P(AXES),
        P(None, AXES),
        P(None, AXES),
    )
    out_specs = (P(AXES, None), P(AXES, None))
    return jax.shard_map(body, mesh=mesh, in_specs=in_specs, out_specs=out_specs, check_vma=False)
```

```python
import functools

import jax
import jax.numpy as jnp
from jax import lax
from jax.experimental import pallas as pl
from jax.experimental.pallas import tpu as pltpu
from jax.sharding import PartitionSpec as P

AXES = ("row", "col")
F32, BF16, I16, I32 = jnp.float32, jnp.bfloat16, jnp.int16, jnp.int32
BS = 128
EXTRA = 8
LOG_TOP = 14.997
STEPS = 64.0
LEAST = 1e-30
FINE = 65000.0

ANY = pl.BlockSpec(memory_space=pl.ANY)
SMEM = pl.BlockSpec(memory_space=pltpu.SMEM)
VMEM = pl.BlockSpec(memory_space=pltpu.VMEM)
HBM = pl.BlockSpec(memory_space=pltpu.HBM)


def params(mib):
    return pltpu.CompilerParams(vmem_limit_bytes=mib << 20)


def held(x):
    return pltpu.with_memory_space_constraint(x, pltpu.HBM)


def swap(x):
    cores = lax.axis_size("col")
    return lax.ppermute(x, "col", [(k, k ^ 1) for k in range(cores)])


def exchange(x):
    return lax.all_to_all(x, AXES, split_axis=0, concat_axis=0, tiled=True)


def fetch(hbm, vmem, sems, chunk):
    return [
        pltpu.make_async_copy(
            hbm.at[pl.ds(c * chunk, chunk)], vmem.at[pl.ds(c * chunk, chunk)], sems.at[c]
        )
        for c in range(hbm.shape[0] // chunk)
    ]


def clear_all(acc):
    def clear(g, _):
        acc[g] = jnp.zeros(acc.shape[1:], F32)
        return 0

    lax.fori_loop(0, acc.shape[0], clear, 0, unroll=4)


def run_chunks(copies, group):
    def step(c, _):
        for k, copy in enumerate(copies):

            @pl.when(c == k)
            def _():
                copy.wait()

        group(c)
        return 0

    lax.fori_loop(0, len(copies), step, 0)


def histogram(seeds_ref, out_ref, factor, to_clear=None):
    columns, depth = seeds_ref.shape
    blocks = out_ref.shape[0] // columns
    unroll = 16
    none = jnp.zeros((blocks, depth), BF16)

    steps = columns // (2 * unroll)

    def group(g, _):
        if to_clear is not None:
            part = to_clear.shape[0] // steps
            for u in range(part):
                to_clear[g * part + u] = jnp.zeros(to_clear.shape[1:], F32)
        for u in range(unroll):
            s = (g * unroll + u) * 2
            highs, lows = [], []
            for one in range(2):
                local = seeds_ref[pl.ds(s + one, 1), :] & (blocks * BS - 1)
                highs.append((lax.broadcasted_iota(I32, (blocks, depth), 0) == (local >> 7)).astype(F32).astype(BF16))
                lows.append((lax.broadcasted_iota(I32, (BS, depth), 0) == (local & (BS - 1))).astype(F32).astype(BF16))
            left = jnp.concatenate(
                [jnp.concatenate([highs[0], none], axis=1), jnp.concatenate([none, highs[1]], axis=1)], axis=0
            )
            count = lax.dot_general(
                left, jnp.concatenate(lows, axis=1), (((1,), (1,)), ((), ())), preferred_element_type=F32
            )
            for one in range(2):
                out_ref[pl.ds(s + one, blocks, stride=columns), :] = count[one * blocks : (one + 1) * blocks] * factor
        return 0

    lax.fori_loop(0, steps, group, 0)


def encode_scale(largest):
    return jnp.ceil(jnp.log2(jnp.maximum(largest, LEAST)) * STEPS)


def up(code):
    return jnp.exp2(LOG_TOP - code * (1.0 / STEPS))


def down(code):
    return jnp.exp2(code * (1.0 / STEPS) - LOG_TOP)


def to_i16(x):
    return jnp.round(x).astype(I32).astype(I16)


def push(x_ref, tiles, copies, src, slot, acc):
    unroll = tiles.shape[0] // len(copies)

    def group(g):
        base = g * unroll
        parts = [
            jnp.dot(x_ref[src[base + u]], tiles[base + u], preferred_element_type=F32)
            for u in range(unroll)
        ]
        for u in range(unroll):
            at = slot[base + u]
            acc[at] = acc[at] + parts[u]

    run_chunks(copies, group)


def send(acc, extra_row, staged, out_hbm, sems, chunk, lists=None):
    copies = []
    row = lax.broadcasted_iota(I32, (EXTRA, BS), 0)
    unroll = min(8, chunk)
    for c in range(acc.shape[0] // chunk):

        def group(g, _):
            for u in range(unroll):
                p = c * chunk + g * unroll + u
                block = acc[p]
                code = encode_scale(jnp.max(jnp.abs(block), axis=0, keepdims=True))
                staged[p, 0:BS, :] = to_i16(block * up(code))
                tail = jnp.where(row == 0, jnp.broadcast_to(code.astype(I32), (EXTRA, BS)), extra_row(p))
                staged[p, BS : BS + EXTRA, :] = tail.astype(I16)
                if lists is not None:
                    staged[p, BS + EXTRA :, :] = lists[u % 2]
            return 0

        lax.fori_loop(0, chunk // unroll, group, 0)
        copy = pltpu.make_async_copy(
            staged.at[pl.ds(c * chunk, chunk)], out_hbm.at[pl.ds(c * chunk, chunk)], sems.at[c]
        )
        copy.start()
        copies.append(copy)
    for copy in copies:
        copy.wait()


def receive(arrived, copies, ids, total, chunk, also=None):
    for b in range(total.shape[0]):
        total[b] = jnp.zeros(total.shape[1:], F32)
    unroll = min(16, chunk)
    for c, copy in enumerate(copies):
        if copy is not None:
            copy.wait()
        at_chunk = ids(c)

        def group(g, _):
            for u in range(unroll):
                one = g * unroll + u
                p = c * chunk + one
                tail = arrived[p, BS : BS + EXTRA, :].astype(I32).astype(F32)
                values = arrived[p, 0:BS, :].astype(I32).astype(F32) * down(tail[0:1])
                at = at_chunk(one)
                total[at] = total[at] + values
                if also is not None:
                    also(at, tail)
            return 0

        lax.fori_loop(0, chunk // unroll, group, 0)


def ids_in(ids):
    return lambda c: lambda one: ids[c, 0, one]


def first_kernel(slots_chunk, tiles_chunk, factor, src, slot, slot_block, seeds, spam_turned, degree, tiles_hbm,
                 out_hbm, good, x, tiles, counts, acc, staged, tile_sems, out_sems):
    copies = fetch(tiles_hbm, tiles, tile_sems, tiles_chunk)
    for copy in copies:
        copy.start()
    histogram(seeds, counts, factor, acc)
    blocks, columns = x.shape[0], x.shape[1]

    def scale(b, _):
        trust = counts[pl.ds(b * columns, columns), :]
        good[b] = trust.astype(BF16)
        x[b] = (trust / degree[b].astype(F32)).astype(BF16)
        return 0

    lax.fori_loop(0, blocks, scale, 0, unroll=4)
    push(x, tiles, copies, src, slot, acc)
    local = (spam_turned[...] & (blocks * BS - 1)).astype(I16)
    half = local.shape[0] // 2
    lists = (local[0:half], local[half:])
    send(acc, lambda p: slot_block[p], staged, out_hbm, out_sems, slots_chunk, lists)


def second_kernel(slots_chunk, tiles_chunk, src, slot, degree, good, weights, arrived_hbm, tiles_hbm, out_hbm, ids_out,
                  arrived, tiles, x, total, acc, staged, ids, in_sems, tile_sems, id_sems, out_sems):
    incoming = fetch(arrived_hbm, arrived, in_sems, slots_chunk)
    copies = fetch(tiles_hbm, tiles, tile_sems, tiles_chunk)
    for copy in incoming:
        copy.start(priority=0)
    for copy in copies:
        copy.start(priority=1)
    clear_all(acc)
    lane = lax.broadcasted_iota(I32, (1, BS), 1)
    moves = []

    def collect(c):
        incoming[c].wait()
        row = jnp.zeros((1, BS), I32)
        for u in range(slots_chunk):
            tail = arrived[c * slots_chunk + u, BS : BS + EXTRA, :].astype(I32)
            row = jnp.where(lane == u, tail[1:2], row)
        ids_out[c] = row
        move = pltpu.make_async_copy(ids_out.at[c], ids.at[c], id_sems.at[c])
        move.start()
        moves.append(move)

    chunks = len(incoming)
    for c in range(min(2, chunks)):
        collect(c)

    def ids_of(c):
        if c + 2 < chunks:
            collect(c + 2)
        moves[c].wait()
        return lambda one: ids[c, 0, one]

    receive(arrived, [None] * chunks, ids_of, total, slots_chunk)

    def scale(b, _):
        trust = 0.85 * total[b] + 0.15 * good[b].astype(F32)
        x[b] = (trust / degree[b].astype(F32)).astype(BF16)
        return 0

    lax.fori_loop(0, x.shape[0], scale, 0, unroll=4)
    push(x, tiles, copies, src, slot, acc)
    send(acc, lambda p: weights[p].astype(I32), staged, out_hbm, out_sems, slots_chunk)


def requests(share, ids, staged, out_hbm, sems, chunk):
    copies = []
    unroll = min(16, chunk)
    for c in range(staged.shape[0] // chunk):

        def group(g, _):
            for u in range(unroll):
                one = g * unroll + u
                staged[c * chunk + one] = share[ids[c, 0, one]]
            return 0

        lax.fori_loop(0, chunk // unroll, group, 0)
        copy = pltpu.make_async_copy(
            staged.at[pl.ds(c * chunk, chunk)], out_hbm.at[pl.ds(c * chunk, chunk)], sems.at[c]
        )
        copy.start()
        copies.append(copy)
    for copy in copies:
        copy.wait()


def third_kernel(slots_chunk, ids, good, spam, spam_hosts, arrived_hbm, out_hbm, trust, shield, in_weight,
                 arrived, total, share, staged, in_sems, out_sem):
    incoming = fetch(arrived_hbm, arrived, in_sems, slots_chunk)
    for copy in incoming:
        copy.start()
    blocks, columns = total.shape[0], total.shape[1]
    in_weight[...] = jnp.ones(in_weight.shape, F32)

    def add_weight(at, tail):
        value = (tail[2:3] + tail[3:4] * (1.0 / FINE)) * down(tail[1:2])
        in_weight[at] = in_weight[at] + value

    receive(arrived, incoming, ids_in(ids), total, slots_chunk, add_weight)
    local = spam_hosts[...] & (blocks * BS - 1)
    low, high = local & (BS - 1), local >> 7
    half = columns // 2
    left = lax.broadcasted_iota(I32, low.shape, 1) < BS // 2

    def finish(b, listed):
        value = 0.85 * total[b] + 0.15 * good[b].astype(F32)
        trust[b] = value
        keep = 1.0 / (1.0 + value)
        shield[b] = keep
        part = keep * spam[b].astype(F32) / in_weight[b]
        found = [
            jnp.take_along_axis(p, low, axis=1, mode="promise_in_bounds") for p in (part[0:half], part[half:])
        ]
        return jnp.where(high == b, jnp.where(left, found[0], found[1]), listed)

    listed = lax.fori_loop(0, blocks, finish, jnp.zeros(low.shape, F32), unroll=4)
    share[...] = listed.astype(BF16)
    rows = half // 2
    parts = (share[0:rows], share[rows:])
    for p in range(staged.shape[0]):
        staged[p] = parts[p % 2]
    copy = pltpu.make_async_copy(staged, out_hbm, out_sem)
    copy.start()
    copy.wait()


def two_halves(core, mine_hbm, other_hbm, whole, sems, rows):
    return [
        pltpu.make_async_copy(
            half, whole.at[:, pl.ds(pl.multiple_of(place * rows, rows), rows)], sems.at[n]
        )
        for n, (half, place) in enumerate(((mine_hbm, core[0]), (other_hbm, 1 - core[0])))
    ]


def places_kernel(core, slot_block, mine_hbm, other_hbm, out_hbm, lists, staged, sems, out_sem):
    columns = staged.shape[1]
    depth = lists.shape[1]
    copies = two_halves(core, mine_hbm, other_hbm, lists, sems, depth // 2)
    for copy in copies:
        copy.start()
    for copy in copies:
        copy.wait()
    host = lax.broadcasted_iota(I32, (BS, columns), 0).astype(F32).astype(BF16)
    lower = lax.broadcasted_iota(I32, (columns, BS), 0) >= columns // 2

    def one(q, _):
        offset = lists[q].astype(I32) - slot_block[q] * BS
        offset = offset.astype(F32).astype(BF16)
        at = jnp.full((BS, columns), -1.0, BF16)
        for j in range(depth):
            at = jnp.where(offset[j : j + 1] == host, jnp.array(j, BF16), at)
        place = jnp.transpose(at.astype(F32))
        place = jnp.where(lower & (place >= 0.0), place + float(depth), place)
        staged[q] = place.astype(I32).astype(I16)
        return 0

    lax.fori_loop(0, staged.shape[0], one, 0)
    back = pltpu.make_async_copy(staged, out_hbm, out_sem)
    back.start()
    back.wait()


def pack_kernel(pairs, tiles_hbm, out_hbm, tiles, staged, sem, out_sem):
    copy = pltpu.make_async_copy(tiles_hbm, tiles, sem)
    copy.start()
    copy.wait()
    size = tiles.shape[1]

    def turn(k, _):
        staged[k, 0:size, :] = jnp.transpose(tiles[pairs[1, k]])
        staged[k, size : 2 * size, :] = jnp.transpose(tiles[pairs[2, k]])
        return 0

    lax.fori_loop(0, staged.shape[0], turn, 0)
    back = pltpu.make_async_copy(staged, out_hbm, out_sem)
    back.start()
    back.wait()


def before_pull(y, total):
    y[y.shape[0] - 1] = jnp.zeros(y.shape[1:], BF16)
    clear_all(total)


def pull(pairs, y, packed, copies, total):
    unroll = packed.shape[0] // len(copies)

    def group(g):
        parts = []
        for u in range(unroll):
            k = g * unroll + u
            left = jnp.concatenate([y[pairs[3, k]], y[pairs[4, k]]], axis=1)
            parts.append(jnp.dot(left, packed[k], preferred_element_type=F32))
        for u in range(unroll):
            at = pairs[0, g * unroll + u]
            total[at] = total[at] + parts[u]

    run_chunks(copies, group)


def place_copies(at_core, places_hbm, places, sems):
    rows = places.shape[1] // 2
    half = places_hbm.shape[1] // 2
    chunks = sems.shape[0]
    size = places.shape[0] // chunks
    first = pl.multiple_of(at_core * rows, rows)
    return [
        [
            pltpu.make_async_copy(
                places_hbm.at[pl.ds(c * size, size), pl.ds(h * half + first, rows)],
                places.at[pl.ds(c * size, size), h * rows : (h + 1) * rows],
                sems.at[c, h],
            )
            for h in range(2)
        ]
        for c in range(chunks)
    ]


def expand(values, places, copies, store):
    rows = values.shape[1]
    size = values.shape[0] // len(copies)
    unroll = min(16, size)
    for c, pair in enumerate(copies):
        for copy in pair:
            copy.wait()

        def group(g, _):
            for u in range(unroll):
                q = c * size + g * unroll + u
                value = values[q].astype(F32)
                for h in range(2):
                    place = places[q, h * rows : (h + 1) * rows, :].astype(I32)
                    found = jnp.take_along_axis(value, jnp.maximum(place, 0), axis=1, mode="promise_in_bounds")
                    store(q, h, jnp.where(place >= 0, found, 0.0).astype(BF16))
            return 0

        lax.fori_loop(0, size // unroll, group, 0)


def own_kernel(core, mine_hbm, places_hbm, part, values, places, sem, place_sems):
    value_copy = pltpu.make_async_copy(mine_hbm, values, sem)
    value_copy.start()
    copies = place_copies(core[0], places_hbm, places, place_sems)
    for pair in copies:
        for copy in pair:
            copy.start()
    value_copy.wait()
    rows = values.shape[1]

    def store(q, h, found):
        part[q, h * rows : (h + 1) * rows, :] = found

    expand(values, places, copies, store)


def fourth_kernel(slots_chunk, core, ids, pairs, spam, shield, in_weight, part, other_hbm, places_hbm, packed_hbm,
                  out_hbm, values, places, y, packed, total, share, staged, sem, place_sems, pair_sems, out_sems):
    value_copy = pltpu.make_async_copy(other_hbm, values, sem)
    value_copy.start(priority=0)
    places_in = place_copies(1 - core[0], places_hbm, places, place_sems)
    for pair in places_in:
        for copy in pair:
            copy.start(priority=0)
    copies = fetch(packed_hbm, packed, pair_sems, packed.shape[0] // pair_sems.shape[0])
    for copy in copies:
        copy.start(priority=1)
    before_pull(y, total)
    rows = values.shape[1]
    half = y.shape[1] // 2
    here = pl.multiple_of(core[0] * rows, rows)
    there = pl.multiple_of((1 - core[0]) * rows, rows)
    value_copy.wait()

    def store(q, h, found):
        y[q, pl.ds(h * half + there, rows), :] = found
        y[q, pl.ds(h * half + here, rows), :] = part[q, h * rows : (h + 1) * rows, :]

    expand(values, places, places_in, store)
    pull(pairs, y, packed, copies, total)

    def finish(b, _):
        value = 0.85 * total[b] + 0.15 * spam[b].astype(F32)
        share[b] = (shield[b] * value / in_weight[b]).astype(BF16)
        return 0

    lax.fori_loop(0, share.shape[0], finish, 0, unroll=4)
    requests(share, ids, staged, out_hbm, out_sems, slots_chunk)


def fifth_kernel(slots_chunk, pairs, spam, arrived_hbm, packed_hbm, out_hbm, y, packed, total, distrust, in_sems, pair_sems, out_sems):
    incoming = fetch(arrived_hbm, y, in_sems, slots_chunk)
    copies = fetch(packed_hbm, packed, pair_sems, packed.shape[0] // pair_sems.shape[0])
    for copy in incoming:
        copy.start(priority=0)
    for copy in copies:
        copy.start(priority=1)
    before_pull(y, total)
    for copy in incoming:
        copy.wait()
    pull(pairs, y, packed, copies, total)

    def finish(b, _):
        distrust[b] = jnp.transpose(0.85 * total[b] + 0.15 * spam[b].astype(F32))
        return 0

    part = total.shape[0] // out_sems.shape[0]
    back = fetch(distrust, out_hbm, out_sems, part)
    for n, copy in enumerate(back):
        lax.fori_loop(n * part, (n + 1) * part, finish, 0, unroll=4)
        copy.start()
    for copy in back:
        copy.wait()


def turn_kernel(wide, tall):
    def turn(b, _):
        tall[b] = jnp.transpose(wide[b])
        return 0

    lax.fori_loop(0, wide.shape[0], turn, 0)


def side_kernel(factor, seeds, slot, tiles_hbm, spam, weights, tiles, counts, sums, sem):
    copy = pltpu.make_async_copy(tiles_hbm, tiles, sem)
    copy.start()
    histogram(seeds, counts, factor)
    blocks, columns = spam.shape[0], spam.shape[1]

    def keep(b, _):
        spam[b] = counts[pl.ds(b * columns, columns), :].astype(BF16)
        return 0

    lax.fori_loop(0, blocks, keep, 0)
    copy.wait()
    sums[...] = jnp.zeros(sums.shape, F32)
    unroll = 4

    def group(g, _):
        for u in range(unroll):
            k = g * unroll + u
            at = slot[k]
            sums[at] = sums[at] + jnp.sum(tiles[k].astype(F32), axis=0, keepdims=True)
        return 0

    lax.fori_loop(0, tiles.shape[0] // unroll, group, 0)
    row = lax.broadcasted_iota(I32, (EXTRA, BS), 0)

    def pack(p, _):
        value = sums[p]
        code = encode_scale(jnp.abs(value))
        whole = value * up(code)
        coarse = jnp.round(whole)
        fine = jnp.round((whole - coarse) * FINE)
        wide = lambda v: jnp.broadcast_to(v, (EXTRA, BS)).astype(I32)
        tail = jnp.where(row == 1, wide(code), jnp.where(row == 2, wide(coarse), jnp.where(row == 3, wide(fine), 0)))
        weights[p] = tail.astype(I16)
        return 0

    lax.fori_loop(0, sums.shape[0], pack, 0)


def cost(flops, bytes_moved):
    return pl.CostEstimate(flops=flops, bytes_accessed=bytes_moved, transcendentals=0)


def pair_up(tile_src, tile_slot, blocks, slots):
    count = tile_src.shape[0]
    pairs = (count + blocks) // 2
    k = jnp.arange(count, dtype=I32)
    same = tile_src[:, None] == tile_src[None, :]
    rank = jnp.sum((same & (k[None, :] < k[:, None])).astype(I32), axis=1)
    block = jnp.arange(blocks, dtype=I32)
    held = jnp.sum((tile_src[:, None] == block[None, :]).astype(I32), axis=0)
    halves = (held + 1) // 2
    first = jnp.sum(jnp.where(block[:, None] < block[None, :], halves[:, None], 0), axis=0)
    start = jnp.sum(jnp.where(tile_src[:, None] == block[None, :], first[None, :], 0), axis=1)
    place = start + rank // 2
    here = place[None, :] == jnp.arange(pairs, dtype=I32)[:, None]
    even = here & (rank % 2 == 0)[None, :]
    odd = here & (rank % 2 == 1)[None, :]
    pick = lambda mask, v: jnp.sum(jnp.where(mask, v[None, :], 0), axis=1)
    shifted = tile_slot - slots
    return jnp.stack(
        [pick(even, tile_src), pick(even, k), pick(odd, k), slots + pick(even, shifted), slots + pick(odd, shifted)]
    )


def cost(flops, bytes_moved):
    return pl.CostEstimate(flops=flops, bytes_accessed=bytes_moved, transcendentals=0)


def body(tiles, tile_src, tile_slot, slot_block, out_degree, good_seeds, spam_cores):
    count, size = tiles.shape[0], tiles.shape[1]
    hosts = out_degree.shape[0]
    blocks = hosts // size
    columns = good_seeds.shape[0]
    slots = slot_block.shape[0]
    slots_chunk = min(16, slots)
    chunks = slots // slots_chunk
    sems = pltpu.SemaphoreType.DMA((chunks,))
    sds = jax.ShapeDtypeStruct
    sent = pltpu.HBM((slots, columns + EXTRA, size), I16)
    asked = pltpu.HBM((slots, columns, size), BF16)
    ids_shape = sds((chunks, 1, size), I32)
    panel = (blocks, columns, size)
    sent_buf = pltpu.VMEM(sent.shape, I16)
    asked_buf = pltpu.VMEM(asked.shape, BF16)
    y_buf = pltpu.VMEM((slots + 1, columns, size), BF16)
    total_buf = pltpu.VMEM(panel, F32)
    half_buf = pltpu.VMEM(panel, BF16)
    acc_buf = pltpu.VMEM((slots, columns, size), F32)
    counts_buf = pltpu.VMEM((blocks * columns, size), F32)
    degree = out_degree.reshape(blocks, 1, size)
    work = 2 * count * size * size * columns
    tile_bytes = 2 * count * size * size
    tiles_chunk = min(128, count)
    tiles_buf = pltpu.VMEM(tiles.shape, BF16)
    tile_sems = pltpu.SemaphoreType.DMA((count // tiles_chunk,))
    couples = (count + blocks) // 2
    pair_sems = pltpu.SemaphoreType.DMA((next(n for n in (4, 5, 2, 1) if couples % n == 0),))
    packed_shape = (couples, 2 * size, size)
    packed_buf = pltpu.VMEM(packed_shape, BF16)

    depth = spam_cores.shape[1]
    half = depth // 2
    first_sent = (slots, columns + EXTRA + half, size)
    outgoing, good = pl.pallas_call(
        functools.partial(first_kernel, slots_chunk, tiles_chunk, float(hosts / good_seeds.shape[1])),
        out_shape=(pltpu.HBM(first_sent, I16), sds(panel, BF16)),
        in_specs=[SMEM, SMEM, SMEM, VMEM, VMEM, VMEM, ANY],
        out_specs=(HBM, VMEM),
        scratch_shapes=[half_buf, tiles_buf, counts_buf, acc_buf, pltpu.VMEM(first_sent, I16), tile_sems, sems],
        compiler_params=params(57),
        cost_estimate=cost(work, 2 * tile_bytes),
        name="first_push",
    )(tile_src, tile_slot, slot_block, good_seeds, spam_cores.T, degree, held(tiles))
    arrived = exchange(outgoing)
    spam_seeds, src_after, slot_after, _ = lax.optimization_barrier((spam_cores, tile_src, tile_slot, outgoing))
    spam_hosts = jnp.concatenate([spam_seeds[: columns // 2], spam_seeds[columns // 2 :]], axis=1)
    spam, weights = pl.pallas_call(
        functools.partial(side_kernel, float(hosts / spam_cores.shape[1])),
        out_shape=(sds(panel, BF16), sds((slots, EXTRA, size), I16)),
        in_specs=[VMEM, SMEM, ANY],
        out_specs=(VMEM, VMEM),
        scratch_shapes=[tiles_buf, counts_buf, pltpu.VMEM((slots, 1, size), F32), pltpu.SemaphoreType.DMA],
        compiler_params=params(40),
        cost_estimate=cost(work // 4, tile_bytes),
        name="side",
    )(spam_seeds, slot_after, held(tiles))
    pairs = pair_up(src_after, slot_after, blocks, slots)
    pair_tiles = lax.optimization_barrier((pairs, outgoing))[0]
    packed = pl.pallas_call(
        pack_kernel,
        out_shape=pltpu.HBM(packed_shape, BF16),
        in_specs=[SMEM, ANY],
        out_specs=HBM,
        scratch_shapes=[tiles_buf, packed_buf, pltpu.SemaphoreType.DMA, pltpu.SemaphoreType.DMA],
        compiler_params=params(40),
        cost_estimate=cost(work // 4, 2 * tile_bytes),
        name="pack",
    )(pair_tiles, held(tiles))
    arrived, packed, weights = lax.optimization_barrier((arrived, packed, weights))
    outgoing, ids = pl.pallas_call(
        functools.partial(second_kernel, slots_chunk, tiles_chunk),
        out_shape=(sent, ids_shape),
        in_specs=[SMEM, SMEM, VMEM, VMEM, VMEM, HBM, ANY],
        out_specs=(HBM, VMEM),
        scratch_shapes=[
            pltpu.VMEM(first_sent, I16), tiles_buf, half_buf, total_buf, acc_buf, sent_buf,
            pltpu.SMEM(ids_shape.shape, I32), sems, tile_sems, sems, sems,
        ],
        compiler_params=params(40),
        cost_estimate=cost(work, 2 * tile_bytes),
        name="second_push",
    )(tile_src, tile_slot, degree, good, weights, held(arrived), held(tiles))
    first_arrived, _ = lax.optimization_barrier((arrived, outgoing))
    arrived = exchange(outgoing)
    core = (lax.axis_index("col") % 2).astype(I32)[None]
    mine = first_arrived[:, columns + EXTRA :, :]
    places = pl.pallas_call(
        places_kernel,
        out_shape=pltpu.HBM((slots, columns, size), I16),
        in_specs=[SMEM, SMEM, ANY, ANY],
        out_specs=HBM,
        scratch_shapes=[
            pltpu.VMEM((slots, depth, size), I16), pltpu.VMEM((slots, columns, size), I16),
            pltpu.SemaphoreType.DMA((2,)), pltpu.SemaphoreType.DMA,
        ],
        compiler_params=params(40),
        cost_estimate=cost(work, tile_bytes),
        name="places",
    )(core, slot_block, mine, swap(mine))
    arrived, places = lax.optimization_barrier((arrived, places))
    listed_shape = (slots, columns // 4, size)
    outgoing, trust, shield, in_weight = pl.pallas_call(
        functools.partial(third_kernel, slots_chunk),
        out_shape=(pltpu.HBM(listed_shape, BF16), sds(panel, F32), sds(panel, F32), sds((blocks, 1, size), F32)),
        in_specs=[SMEM, VMEM, VMEM, VMEM, HBM],
        out_specs=(HBM, VMEM, VMEM, VMEM),
        scratch_shapes=[
            sent_buf, total_buf, pltpu.VMEM((columns // 2, size), BF16), pltpu.VMEM(listed_shape, BF16),
            sems, pltpu.SemaphoreType.DMA,
        ],
        compiler_params=params(40),
        cost_estimate=cost(work // 8, tile_bytes),
        name="first_shares",
    )(ids, good, spam, spam_hosts, held(arrived))
    mine = exchange(outgoing)
    trust_out = pl.pallas_call(
        turn_kernel,
        out_shape=sds((blocks, size, columns), F32),
        in_specs=[VMEM],
        out_specs=VMEM,
        compiler_params=params(16),
        cost_estimate=cost(work // 64, tile_bytes // 4),
        name="turn",
    )(trust)
    quarter_buf = pltpu.VMEM(listed_shape, BF16)
    places_buf = pltpu.VMEM((slots, columns // 2, size), I16)
    place_sems = pltpu.SemaphoreType.DMA((min(4, chunks), 2))
    part = pl.pallas_call(
        own_kernel,
        out_shape=sds((slots, columns // 2, size), BF16),
        in_specs=[SMEM, ANY, HBM],
        out_specs=VMEM,
        scratch_shapes=[quarter_buf, places_buf, pltpu.SemaphoreType.DMA, place_sems],
        compiler_params=params(24),
        cost_estimate=cost(work // 4, tile_bytes // 2),
        name="own_values",
    )(core, mine, held(places))
    asked_for = pl.pallas_call(
        functools.partial(fourth_kernel, slots_chunk),
        out_shape=asked,
        in_specs=[SMEM, SMEM, SMEM, VMEM, VMEM, VMEM, VMEM, ANY, HBM, HBM],
        out_specs=HBM,
        scratch_shapes=[
            quarter_buf, places_buf, y_buf, packed_buf, total_buf, half_buf, asked_buf,
            pltpu.SemaphoreType.DMA, place_sems, pair_sems, sems,
        ],
        compiler_params=params(44),
        cost_estimate=cost(work, 2 * tile_bytes),
        name="second_shares",
    )(core, ids, pairs, spam, shield, in_weight, part, swap(mine), held(places), held(packed))
    arrived = exchange(asked_for)
    distrust = pl.pallas_call(
        functools.partial(fifth_kernel, slots_chunk),
        out_shape=pltpu.HBM((blocks, size, columns), F32),
        in_specs=[SMEM, VMEM, HBM, HBM],
        out_specs=HBM,
        scratch_shapes=[
            y_buf, packed_buf, total_buf, pltpu.VMEM((blocks, size, columns), F32), sems, pair_sems,
            pltpu.SemaphoreType.DMA((blocks // 4,)),
        ],
        compiler_params=params(40),
        cost_estimate=cost(work, 2 * tile_bytes),
        name="last_pull",
    )(pairs, spam, held(arrived), held(packed))
    return trust_out.reshape(hosts, columns), distrust.reshape(hosts, columns)


def solution(mesh):
    in_specs = (
        P(AXES, None, None),
        P(AXES),
        P(AXES),
        P(AXES),
        P(AXES),
        P(None, AXES),
        P(None, AXES),
    )
    out_specs = (P(AXES, None), P(AXES, None))
    return jax.shard_map(body, mesh=mesh, in_specs=in_specs, out_specs=out_specs, check_vma=False)
```

```python
import functools

import jax
import jax.numpy as jnp
from jax import lax
from jax.experimental import pallas as pl
from jax.experimental.pallas import tpu as pltpu
from jax.sharding import PartitionSpec as P

AXES = ("row", "col")
F32, BF16, I16, I32 = jnp.float32, jnp.bfloat16, jnp.int16, jnp.int32
BS = 128
EXTRA = 8
LOG_TOP = 14.997
STEPS = 64.0
LEAST = 1e-30
FINE = 65000.0

ANY = pl.BlockSpec(memory_space=pl.ANY)
SMEM = pl.BlockSpec(memory_space=pltpu.SMEM)
VMEM = pl.BlockSpec(memory_space=pltpu.VMEM)
HBM = pl.BlockSpec(memory_space=pltpu.HBM)


def params(mib):
    return pltpu.CompilerParams(vmem_limit_bytes=mib << 20)


def held(x):
    return pltpu.with_memory_space_constraint(x, pltpu.HBM)


def swap(x):
    cores = lax.axis_size("col")
    return lax.ppermute(x, "col", [(k, k ^ 1) for k in range(cores)])


def exchange(x):
    return lax.all_to_all(x, AXES, split_axis=0, concat_axis=0, tiled=True)


def fetch(hbm, vmem, sems, chunk):
    return [
        pltpu.make_async_copy(
            hbm.at[pl.ds(c * chunk, chunk)], vmem.at[pl.ds(c * chunk, chunk)], sems.at[c]
        )
        for c in range(hbm.shape[0] // chunk)
    ]


def clear_all(acc):
    def clear(g, _):
        acc[g] = jnp.zeros(acc.shape[1:], F32)
        return 0

    lax.fori_loop(0, acc.shape[0], clear, 0, unroll=4)


def run_chunks(copies, group):
    def step(c, _):
        for k, copy in enumerate(copies):

            @pl.when(c == k)
            def _():
                copy.wait()

        group(c)
        return 0

    lax.fori_loop(0, len(copies), step, 0)


def histogram(seeds_ref, out_ref, factor, to_clear=None):
    columns, depth = seeds_ref.shape
    blocks = out_ref.shape[0] // columns
    unroll = 16
    none = jnp.zeros((blocks, depth), BF16)

    steps = columns // (2 * unroll)

    def group(g, _):
        if to_clear is not None:
            part = to_clear.shape[0] // steps
            for u in range(part):
                to_clear[g * part + u] = jnp.zeros(to_clear.shape[1:], F32)
        for u in range(unroll):
            s = (g * unroll + u) * 2
            highs, lows = [], []
            for one in range(2):
                local = seeds_ref[pl.ds(s + one, 1), :] & (blocks * BS - 1)
                highs.append((lax.broadcasted_iota(I32, (blocks, depth), 0) == (local >> 7)).astype(F32).astype(BF16))
                lows.append((lax.broadcasted_iota(I32, (BS, depth), 0) == (local & (BS - 1))).astype(F32).astype(BF16))
            left = jnp.concatenate(
                [jnp.concatenate([highs[0], none], axis=1), jnp.concatenate([none, highs[1]], axis=1)], axis=0
            )
            count = lax.dot_general(
                left, jnp.concatenate(lows, axis=1), (((1,), (1,)), ((), ())), preferred_element_type=F32
            )
            for one in range(2):
                out_ref[pl.ds(s + one, blocks, stride=columns), :] = count[one * blocks : (one + 1) * blocks] * factor
        return 0

    lax.fori_loop(0, steps, group, 0)


def encode_scale(largest):
    return jnp.ceil(jnp.log2(jnp.maximum(largest, LEAST)) * STEPS)


def up(code):
    return jnp.exp2(LOG_TOP - code * (1.0 / STEPS))


def down(code):
    return jnp.exp2(code * (1.0 / STEPS) - LOG_TOP)


def to_i16(x):
    return jnp.round(x).astype(I32).astype(I16)


def push(x_ref, tiles, copies, src, slot, acc):
    unroll = tiles.shape[0] // len(copies)

    def group(g):
        base = g * unroll
        parts = [
            jnp.dot(x_ref[src[base + u]], tiles[base + u], preferred_element_type=F32)
            for u in range(unroll)
        ]
        for u in range(unroll):
            at = slot[base + u]
            acc[at] = acc[at] + parts[u]

    run_chunks(copies, group)


def send(acc, extra_row, staged, out_hbm, sems, chunk, lists=None):
    copies = []
    last = staged.shape[1] - EXTRA
    row = lax.broadcasted_iota(I32, (EXTRA, BS), 0)
    unroll = min(8, chunk)
    for c in range(acc.shape[0] // chunk):

        def group(g, _):
            for u in range(unroll):
                p = c * chunk + g * unroll + u
                block = acc[p]
                code = encode_scale(jnp.max(jnp.abs(block), axis=0, keepdims=True))
                staged[p, 0:BS, :] = to_i16(block * up(code))
                tail = jnp.where(row == 0, jnp.broadcast_to(code.astype(I32), (EXTRA, BS)), extra_row(p))
                staged[p, last:, :] = tail.astype(I16)
                if lists is not None:
                    staged[p, BS:last, :] = lists[u % 2]
            return 0

        lax.fori_loop(0, chunk // unroll, group, 0)
        copy = pltpu.make_async_copy(
            staged.at[pl.ds(c * chunk, chunk)], out_hbm.at[pl.ds(c * chunk, chunk)], sems.at[c]
        )
        copy.start()
        copies.append(copy)
    for copy in copies:
        copy.wait()


def receive(arrived, copies, ids, total, chunk, also=None):
    last = arrived.shape[1] - EXTRA
    for b in range(total.shape[0]):
        total[b] = jnp.zeros(total.shape[1:], F32)
    unroll = min(16, chunk)
    for c, copy in enumerate(copies):
        if copy is not None:
            copy.wait()
        at_chunk = ids(c)

        def group(g, _):
            for u in range(unroll):
                one = g * unroll + u
                p = c * chunk + one
                tail = arrived[p, last:, :].astype(I32).astype(F32)
                values = arrived[p, 0:BS, :].astype(I32).astype(F32) * down(tail[0:1])
                at = at_chunk(one)
                total[at] = total[at] + values
                if also is not None:
                    also(at, tail)
            return 0

        lax.fori_loop(0, chunk // unroll, group, 0)


def ids_in(ids):
    return lambda c: lambda one: ids[c, 0, one]


def first_kernel(slots_chunk, tiles_chunk, factor, src, slot, slot_block, seeds, spam_turned, degree, tiles_hbm,
                 out_hbm, good, x, tiles, counts, acc, staged, tile_sems, out_sems):
    copies = fetch(tiles_hbm, tiles, tile_sems, tiles_chunk)
    for copy in copies:
        copy.start()
    histogram(seeds, counts, factor, acc)
    blocks, columns = x.shape[0], x.shape[1]

    def scale(b, _):
        trust = counts[pl.ds(b * columns, columns), :]
        good[b] = trust.astype(BF16)
        x[b] = (trust / degree[b].astype(F32)).astype(BF16)
        return 0

    lax.fori_loop(0, blocks, scale, 0, unroll=4)
    push(x, tiles, copies, src, slot, acc)
    local = (spam_turned[...] & (blocks * BS - 1)).astype(I16)
    half = local.shape[0] // 2
    lists = (local[0:half], local[half:])
    send(acc, lambda p: slot_block[p], staged, out_hbm, out_sems, slots_chunk, lists)


def second_kernel(slots_chunk, tiles_chunk, src, slot, degree, good, weights, arrived_hbm, tiles_hbm, out_hbm, ids_out,
                  arrived, tiles, x, total, acc, staged, ids, in_sems, tile_sems, id_sems, out_sems):
    incoming = fetch(arrived_hbm, arrived, in_sems, slots_chunk)
    copies = fetch(tiles_hbm, tiles, tile_sems, tiles_chunk)
    for copy in incoming:
        copy.start(priority=0)
    for copy in copies:
        copy.start(priority=1)
    clear_all(acc)
    lane = lax.broadcasted_iota(I32, (1, BS), 1)
    moves = []

    def collect(c):
        incoming[c].wait()
        row = jnp.zeros((1, BS), I32)
        for u in range(slots_chunk):
            tail = arrived[c * slots_chunk + u, arrived.shape[1] - EXTRA :, :].astype(I32)
            row = jnp.where(lane == u, tail[1:2], row)
        ids_out[c] = row
        move = pltpu.make_async_copy(ids_out.at[c], ids.at[c], id_sems.at[c])
        move.start()
        moves.append(move)

    chunks = len(incoming)
    for c in range(min(2, chunks)):
        collect(c)

    def ids_of(c):
        if c + 2 < chunks:
            collect(c + 2)
        moves[c].wait()
        return lambda one: ids[c, 0, one]

    receive(arrived, [None] * chunks, ids_of, total, slots_chunk)

    def scale(b, _):
        trust = 0.85 * total[b] + 0.15 * good[b].astype(F32)
        x[b] = (trust / degree[b].astype(F32)).astype(BF16)
        return 0

    lax.fori_loop(0, x.shape[0], scale, 0, unroll=4)
    push(x, tiles, copies, src, slot, acc)
    send(acc, lambda p: weights[p].astype(I32), staged, out_hbm, out_sems, slots_chunk)


def requests(share, ids, staged, out_hbm, sems, chunk):
    copies = []
    unroll = min(16, chunk)
    for c in range(staged.shape[0] // chunk):

        def group(g, _):
            for u in range(unroll):
                one = g * unroll + u
                staged[c * chunk + one] = share[ids[c, 0, one]]
            return 0

        lax.fori_loop(0, chunk // unroll, group, 0)
        copy = pltpu.make_async_copy(
            staged.at[pl.ds(c * chunk, chunk)], out_hbm.at[pl.ds(c * chunk, chunk)], sems.at[c]
        )
        copy.start()
        copies.append(copy)
    for copy in copies:
        copy.wait()


def third_kernel(slots_chunk, ids, good, spam, spam_hosts, arrived_hbm, out_hbm, trust, shield, in_weight,
                 arrived, total, share, staged, in_sems, out_sem):
    incoming = fetch(arrived_hbm, arrived, in_sems, slots_chunk)
    for copy in incoming:
        copy.start()
    blocks, columns = total.shape[0], total.shape[1]
    in_weight[...] = jnp.ones(in_weight.shape, F32)

    def add_weight(at, tail):
        value = (tail[2:3] + tail[3:4] * (1.0 / FINE)) * down(tail[1:2])
        in_weight[at] = in_weight[at] + value

    receive(arrived, incoming, ids_in(ids), total, slots_chunk, add_weight)
    local = spam_hosts[...] & (blocks * BS - 1)
    low, high = local & (BS - 1), local >> 7
    half = columns // 2
    left = lax.broadcasted_iota(I32, low.shape, 1) < BS // 2

    def finish(b, listed):
        value = 0.85 * total[b] + 0.15 * good[b].astype(F32)
        trust[b] = value
        keep = 1.0 / (1.0 + value)
        shield[b] = keep
        part = keep * spam[b].astype(F32) / in_weight[b]
        found = [
            jnp.take_along_axis(p, low, axis=1, mode="promise_in_bounds") for p in (part[0:half], part[half:])
        ]
        return jnp.where(high == b, jnp.where(left, found[0], found[1]), listed)

    listed = lax.fori_loop(0, blocks, finish, jnp.zeros(low.shape, F32), unroll=4)
    share[...] = listed.astype(BF16)
    rows = half // 2
    parts = (share[0:rows], share[rows:])
    for p in range(staged.shape[0]):
        staged[p] = parts[p % 2]
    copy = pltpu.make_async_copy(staged, out_hbm, out_sem)
    copy.start()
    copy.wait()


def two_halves(core, mine_hbm, other_hbm, whole, sems, rows):
    return [
        pltpu.make_async_copy(
            half, whole.at[:, pl.ds(pl.multiple_of(place * rows, rows), rows)], sems.at[n]
        )
        for n, (half, place) in enumerate(((mine_hbm, core[0]), (other_hbm, 1 - core[0])))
    ]


def places_kernel(core, slot_block, mine_hbm, other_hbm, out_hbm, lists, staged, sems, out_sem):
    columns = staged.shape[1]
    depth = lists.shape[1]
    copies = two_halves(core, mine_hbm, other_hbm, lists, sems, depth // 2)
    for copy in copies:
        copy.start()
    for copy in copies:
        copy.wait()
    host = lax.broadcasted_iota(I32, (BS, columns), 0).astype(F32).astype(BF16)
    lower = lax.broadcasted_iota(I32, (columns, BS), 0) >= columns // 2

    def one(q, _):
        offset = lists[q].astype(I32) - slot_block[q] * BS
        offset = offset.astype(F32).astype(BF16)
        at = jnp.full((BS, columns), -1.0, BF16)
        for j in range(depth):
            at = jnp.where(offset[j : j + 1] == host, jnp.array(j, BF16), at)
        place = jnp.transpose(at.astype(F32))
        place = jnp.where(lower & (place >= 0.0), place + float(depth), place)
        staged[q] = place.astype(I32).astype(I16)
        return 0

    lax.fori_loop(0, staged.shape[0], one, 0)
    back = pltpu.make_async_copy(staged, out_hbm, out_sem)
    back.start()
    back.wait()


def pack_kernel(pairs, tiles_hbm, out_hbm, tiles, staged, sem, out_sem):
    copy = pltpu.make_async_copy(tiles_hbm, tiles, sem)
    copy.start()
    copy.wait()
    size = tiles.shape[1]

    def turn(k, _):
        staged[k, 0:size, :] = jnp.transpose(tiles[pairs[1, k]])
        staged[k, size : 2 * size, :] = jnp.transpose(tiles[pairs[2, k]])
        return 0

    lax.fori_loop(0, staged.shape[0], turn, 0)
    back = pltpu.make_async_copy(staged, out_hbm, out_sem)
    back.start()
    back.wait()


def before_pull(y, total):
    y[y.shape[0] - 1] = jnp.zeros(y.shape[1:], BF16)
    clear_all(total)


def pull(pairs, y, packed, copies, total):
    unroll = packed.shape[0] // len(copies)

    def group(g):
        parts = []
        for u in range(unroll):
            k = g * unroll + u
            left = jnp.concatenate([y[pairs[3, k]], y[pairs[4, k]]], axis=1)
            parts.append(jnp.dot(left, packed[k], preferred_element_type=F32))
        for u in range(unroll):
            at = pairs[0, g * unroll + u]
            total[at] = total[at] + parts[u]

    run_chunks(copies, group)


def place_copies(at_core, places_hbm, places, sems):
    rows = places.shape[1] // 2
    half = places_hbm.shape[1] // 2
    chunks = sems.shape[0]
    size = places.shape[0] // chunks
    first = pl.multiple_of(at_core * rows, rows)
    return [
        [
            pltpu.make_async_copy(
                places_hbm.at[pl.ds(c * size, size), pl.ds(h * half + first, rows)],
                places.at[pl.ds(c * size, size), h * rows : (h + 1) * rows],
                sems.at[c, h],
            )
            for h in range(2)
        ]
        for c in range(chunks)
    ]


def expand(values, places, copies, store):
    rows = values.shape[1]
    size = values.shape[0] // len(copies)
    unroll = min(16, size)
    for c, pair in enumerate(copies):
        for copy in pair:
            copy.wait()

        def group(g, _):
            for u in range(unroll):
                q = c * size + g * unroll + u
                value = values[q].astype(F32)
                for h in range(2):
                    place = places[q, h * rows : (h + 1) * rows, :].astype(I32)
                    found = jnp.take_along_axis(value, jnp.maximum(place, 0), axis=1, mode="promise_in_bounds")
                    store(q, h, jnp.where(place >= 0, found, 0.0).astype(BF16))
            return 0

        lax.fori_loop(0, size // unroll, group, 0)


def own_kernel(core, mine_hbm, places_hbm, part, values, places, sem, place_sems):
    value_copy = pltpu.make_async_copy(mine_hbm, values, sem)
    value_copy.start()
    copies = place_copies(core[0], places_hbm, places, place_sems)
    for pair in copies:
        for copy in pair:
            copy.start()
    value_copy.wait()
    rows = values.shape[1]

    def store(q, h, found):
        part[q, h * rows : (h + 1) * rows, :] = found

    expand(values, places, copies, store)


def fourth_kernel(slots_chunk, core, ids, pairs, spam, shield, in_weight, part, other_hbm, places_hbm, packed_hbm,
                  out_hbm, values, places, y, packed, total, share, staged, sem, place_sems, pair_sems, out_sems):
    value_copy = pltpu.make_async_copy(other_hbm, values, sem)
    value_copy.start(priority=0)
    places_in = place_copies(1 - core[0], places_hbm, places, place_sems)
    for pair in places_in:
        for copy in pair:
            copy.start(priority=0)
    copies = fetch(packed_hbm, packed, pair_sems, packed.shape[0] // pair_sems.shape[0])
    for copy in copies:
        copy.start(priority=1)
    before_pull(y, total)
    rows = values.shape[1]
    half = y.shape[1] // 2
    here = pl.multiple_of(core[0] * rows, rows)
    there = pl.multiple_of((1 - core[0]) * rows, rows)
    value_copy.wait()

    def store(q, h, found):
        y[q, pl.ds(h * half + there, rows), :] = found
        y[q, pl.ds(h * half + here, rows), :] = part[q, h * rows : (h + 1) * rows, :]

    expand(values, places, places_in, store)
    pull(pairs, y, packed, copies, total)

    def finish(b, _):
        value = 0.85 * total[b] + 0.15 * spam[b].astype(F32)
        share[b] = (shield[b] * value / in_weight[b]).astype(BF16)
        return 0

    lax.fori_loop(0, share.shape[0], finish, 0, unroll=4)
    requests(share, ids, staged, out_hbm, out_sems, slots_chunk)


def fifth_kernel(slots_chunk, pairs, spam, arrived_hbm, packed_hbm, out_hbm, y, packed, total, distrust, in_sems, pair_sems, out_sems):
    incoming = fetch(arrived_hbm, y, in_sems, slots_chunk)
    copies = fetch(packed_hbm, packed, pair_sems, packed.shape[0] // pair_sems.shape[0])
    for copy in incoming:
        copy.start(priority=0)
    for copy in copies:
        copy.start(priority=1)
    before_pull(y, total)
    for copy in incoming:
        copy.wait()
    pull(pairs, y, packed, copies, total)

    def finish(b, _):
        distrust[b] = jnp.transpose(0.85 * total[b] + 0.15 * spam[b].astype(F32))
        return 0

    part = total.shape[0] // out_sems.shape[0]
    back = fetch(distrust, out_hbm, out_sems, part)
    for n, copy in enumerate(back):
        lax.fori_loop(n * part, (n + 1) * part, finish, 0, unroll=4)
        copy.start()
    for copy in back:
        copy.wait()


def turn_kernel(wide, tall):
    def turn(b, _):
        tall[b] = jnp.transpose(wide[b])
        return 0

    lax.fori_loop(0, wide.shape[0], turn, 0)


def side_kernel(factor, seeds, slot, tiles_hbm, spam, weights, tiles, counts, sums, sem):
    copy = pltpu.make_async_copy(tiles_hbm, tiles, sem)
    copy.start()
    histogram(seeds, counts, factor)
    blocks, columns = spam.shape[0], spam.shape[1]

    def keep(b, _):
        spam[b] = counts[pl.ds(b * columns, columns), :].astype(BF16)
        return 0

    lax.fori_loop(0, blocks, keep, 0)
    copy.wait()
    sums[...] = jnp.zeros(sums.shape, F32)
    unroll = 4

    def group(g, _):
        for u in range(unroll):
            k = g * unroll + u
            at = slot[k]
            sums[at] = sums[at] + jnp.sum(tiles[k].astype(F32), axis=0, keepdims=True)
        return 0

    lax.fori_loop(0, tiles.shape[0] // unroll, group, 0)
    row = lax.broadcasted_iota(I32, (EXTRA, BS), 0)

    def pack(p, _):
        value = sums[p]
        code = encode_scale(jnp.abs(value))
        whole = value * up(code)
        coarse = jnp.round(whole)
        fine = jnp.round((whole - coarse) * FINE)
        wide = lambda v: jnp.broadcast_to(v, (EXTRA, BS)).astype(I32)
        tail = jnp.where(row == 1, wide(code), jnp.where(row == 2, wide(coarse), jnp.where(row == 3, wide(fine), 0)))
        weights[p] = tail.astype(I16)
        return 0

    lax.fori_loop(0, sums.shape[0], pack, 0)


def cost(flops, bytes_moved):
    return pl.CostEstimate(flops=flops, bytes_accessed=bytes_moved, transcendentals=0)


def pair_up(tile_src, tile_slot, blocks, slots):
    count = tile_src.shape[0]
    pairs = (count + blocks) // 2
    k = jnp.arange(count, dtype=I32)
    same = tile_src[:, None] == tile_src[None, :]
    rank = jnp.sum((same & (k[None, :] < k[:, None])).astype(I32), axis=1)
    block = jnp.arange(blocks, dtype=I32)
    held = jnp.sum((tile_src[:, None] == block[None, :]).astype(I32), axis=0)
    halves = (held + 1) // 2
    first = jnp.sum(jnp.where(block[:, None] < block[None, :], halves[:, None], 0), axis=0)
    start = jnp.sum(jnp.where(tile_src[:, None] == block[None, :], first[None, :], 0), axis=1)
    place = start + rank // 2
    here = place[None, :] == jnp.arange(pairs, dtype=I32)[:, None]
    even = here & (rank % 2 == 0)[None, :]
    odd = here & (rank % 2 == 1)[None, :]
    pick = lambda mask, v: jnp.sum(jnp.where(mask, v[None, :], 0), axis=1)
    shifted = tile_slot - slots
    return jnp.stack(
        [pick(even, tile_src), pick(even, k), pick(odd, k), slots + pick(even, shifted), slots + pick(odd, shifted)]
    )


def cost(flops, bytes_moved):
    return pl.CostEstimate(flops=flops, bytes_accessed=bytes_moved, transcendentals=0)


def body(tiles, tile_src, tile_slot, slot_block, out_degree, good_seeds, spam_cores):
    count, size = tiles.shape[0], tiles.shape[1]
    hosts = out_degree.shape[0]
    blocks = hosts // size
    columns = good_seeds.shape[0]
    slots = slot_block.shape[0]
    slots_chunk = min(16, slots)
    chunks = slots // slots_chunk
    sems = pltpu.SemaphoreType.DMA((chunks,))
    sds = jax.ShapeDtypeStruct
    sent = pltpu.HBM((slots, columns + EXTRA, size), I16)
    asked = pltpu.HBM((slots, columns, size), BF16)
    ids_shape = sds((chunks, 1, size), I32)
    panel = (blocks, columns, size)
    sent_buf = pltpu.VMEM(sent.shape, I16)
    asked_buf = pltpu.VMEM(asked.shape, BF16)
    y_buf = pltpu.VMEM((slots + 1, columns, size), BF16)
    total_buf = pltpu.VMEM(panel, F32)
    half_buf = pltpu.VMEM(panel, BF16)
    acc_buf = pltpu.VMEM((slots, columns, size), F32)
    counts_buf = pltpu.VMEM((blocks * columns, size), F32)
    degree = out_degree.reshape(blocks, 1, size)
    work = 2 * count * size * size * columns
    tile_bytes = 2 * count * size * size
    tiles_chunk = min(128, count)
    tiles_buf = pltpu.VMEM(tiles.shape, BF16)
    tile_sems = pltpu.SemaphoreType.DMA((count // tiles_chunk,))
    couples = (count + blocks) // 2
    pair_sems = pltpu.SemaphoreType.DMA((next(n for n in (4, 5, 2, 1) if couples % n == 0),))
    packed_shape = (couples, 2 * size, size)
    packed_buf = pltpu.VMEM(packed_shape, BF16)

    depth = spam_cores.shape[1]
    half = depth // 2
    first_sent = (slots, columns + EXTRA + half, size)
    outgoing, good = pl.pallas_call(
        functools.partial(first_kernel, slots_chunk, tiles_chunk, float(hosts / good_seeds.shape[1])),
        out_shape=(pltpu.HBM(first_sent, I16), sds(panel, BF16)),
        in_specs=[SMEM, SMEM, SMEM, VMEM, VMEM, VMEM, ANY],
        out_specs=(HBM, VMEM),
        scratch_shapes=[half_buf, tiles_buf, counts_buf, acc_buf, pltpu.VMEM(first_sent, I16), tile_sems, sems],
        compiler_params=params(57),
        cost_estimate=cost(work, 2 * tile_bytes),
        name="first_push",
    )(tile_src, tile_slot, slot_block, good_seeds, spam_cores.T, degree, held(tiles))
    arrived = exchange(outgoing)
    spam_seeds, src_after, slot_after, _ = lax.optimization_barrier((spam_cores, tile_src, tile_slot, outgoing))
    spam_hosts = jnp.concatenate([spam_seeds[: columns // 2], spam_seeds[columns // 2 :]], axis=1)
    spam, weights = pl.pallas_call(
        functools.partial(side_kernel, float(hosts / spam_cores.shape[1])),
        out_shape=(sds(panel, BF16), sds((slots, EXTRA, size), I16)),
        in_specs=[VMEM, SMEM, ANY],
        out_specs=(VMEM, VMEM),
        scratch_shapes=[tiles_buf, counts_buf, pltpu.VMEM((slots, 1, size), F32), pltpu.SemaphoreType.DMA],
        compiler_params=params(40),
        cost_estimate=cost(work // 4, tile_bytes),
        name="side",
    )(spam_seeds, slot_after, held(tiles))
    pairs = pair_up(src_after, slot_after, blocks, slots)
    pair_tiles = lax.optimization_barrier((pairs, outgoing))[0]
    packed = pl.pallas_call(
        pack_kernel,
        out_shape=pltpu.HBM(packed_shape, BF16),
        in_specs=[SMEM, ANY],
        out_specs=HBM,
        scratch_shapes=[tiles_buf, packed_buf, pltpu.SemaphoreType.DMA, pltpu.SemaphoreType.DMA],
        compiler_params=params(40),
        cost_estimate=cost(work // 4, 2 * tile_bytes),
        name="pack",
    )(pair_tiles, held(tiles))
    arrived, packed, weights = lax.optimization_barrier((arrived, packed, weights))
    outgoing, ids = pl.pallas_call(
        functools.partial(second_kernel, slots_chunk, tiles_chunk),
        out_shape=(sent, ids_shape),
        in_specs=[SMEM, SMEM, VMEM, VMEM, VMEM, HBM, ANY],
        out_specs=(HBM, VMEM),
        scratch_shapes=[
            pltpu.VMEM(first_sent, I16), tiles_buf, half_buf, total_buf, acc_buf, sent_buf,
            pltpu.SMEM(ids_shape.shape, I32), sems, tile_sems, sems, sems,
        ],
        compiler_params=params(40),
        cost_estimate=cost(work, 2 * tile_bytes),
        name="second_push",
    )(tile_src, tile_slot, degree, good, weights, held(arrived), held(tiles))
    first_arrived, _ = lax.optimization_barrier((arrived, outgoing))
    arrived = exchange(outgoing)
    core = (lax.axis_index("col") % 2).astype(I32)[None]
    mine = first_arrived[:, columns : columns + half, :]
    places = pl.pallas_call(
        places_kernel,
        out_shape=pltpu.HBM((slots, columns, size), I16),
        in_specs=[SMEM, SMEM, ANY, ANY],
        out_specs=HBM,
        scratch_shapes=[
            pltpu.VMEM((slots, depth, size), I16), pltpu.VMEM((slots, columns, size), I16),
            pltpu.SemaphoreType.DMA((2,)), pltpu.SemaphoreType.DMA,
        ],
        compiler_params=params(40),
        cost_estimate=cost(work, tile_bytes),
        name="places",
    )(core, slot_block, mine, swap(mine))
    arrived, places = lax.optimization_barrier((arrived, places))
    listed_shape = (slots, columns // 4, size)
    outgoing, trust, shield, in_weight = pl.pallas_call(
        functools.partial(third_kernel, slots_chunk),
        out_shape=(pltpu.HBM(listed_shape, BF16), sds(panel, F32), sds(panel, F32), sds((blocks, 1, size), F32)),
        in_specs=[SMEM, VMEM, VMEM, VMEM, HBM],
        out_specs=(HBM, VMEM, VMEM, VMEM),
        scratch_shapes=[
            sent_buf, total_buf, pltpu.VMEM((columns // 2, size), BF16), pltpu.VMEM(listed_shape, BF16),
            sems, pltpu.SemaphoreType.DMA,
        ],
        compiler_params=params(40),
        cost_estimate=cost(work // 8, tile_bytes),
        name="first_shares",
    )(ids, good, spam, spam_hosts, held(arrived))
    mine = exchange(outgoing)
    trust_out = pl.pallas_call(
        turn_kernel,
        out_shape=sds((blocks, size, columns), F32),
        in_specs=[VMEM],
        out_specs=VMEM,
        compiler_params=params(16),
        cost_estimate=cost(work // 64, tile_bytes // 4),
        name="turn",
    )(trust)
    quarter_buf = pltpu.VMEM(listed_shape, BF16)
    places_buf = pltpu.VMEM((slots, columns // 2, size), I16)
    place_sems = pltpu.SemaphoreType.DMA((min(4, chunks), 2))
    part = pl.pallas_call(
        own_kernel,
        out_shape=sds((slots, columns // 2, size), BF16),
        in_specs=[SMEM, ANY, HBM],
        out_specs=VMEM,
        scratch_shapes=[quarter_buf, places_buf, pltpu.SemaphoreType.DMA, place_sems],
        compiler_params=params(24),
        cost_estimate=cost(work // 4, tile_bytes // 2),
        name="own_values",
    )(core, mine, held(places))
    asked_for = pl.pallas_call(
        functools.partial(fourth_kernel, slots_chunk),
        out_shape=asked,
        in_specs=[SMEM, SMEM, SMEM, VMEM, VMEM, VMEM, VMEM, ANY, HBM, HBM],
        out_specs=HBM,
        scratch_shapes=[
            quarter_buf, places_buf, y_buf, packed_buf, total_buf, half_buf, asked_buf,
            pltpu.SemaphoreType.DMA, place_sems, pair_sems, sems,
        ],
        compiler_params=params(44),
        cost_estimate=cost(work, 2 * tile_bytes),
        name="second_shares",
    )(core, ids, pairs, spam, shield, in_weight, part, swap(mine), held(places), held(packed))
    arrived = exchange(asked_for)
    distrust = pl.pallas_call(
        functools.partial(fifth_kernel, slots_chunk),
        out_shape=pltpu.HBM((blocks, size, columns), F32),
        in_specs=[SMEM, VMEM, HBM, HBM],
        out_specs=HBM,
        scratch_shapes=[
            y_buf, packed_buf, total_buf, pltpu.VMEM((blocks, size, columns), F32), sems, pair_sems,
            pltpu.SemaphoreType.DMA((blocks // 4,)),
        ],
        compiler_params=params(40),
        cost_estimate=cost(work, 2 * tile_bytes),
        name="last_pull",
    )(pairs, spam, held(arrived), held(packed))
    return trust_out.reshape(hosts, columns), distrust.reshape(hosts, columns)


def solution(mesh):
    in_specs = (
        P(AXES, None, None),
        P(AXES),
        P(AXES),
        P(AXES),
        P(AXES),
        P(None, AXES),
        P(None, AXES),
    )
    out_specs = (P(AXES, None), P(AXES, None))
    return jax.shard_map(body, mesh=mesh, in_specs=in_specs, out_specs=out_specs, check_vma=False)
```
